256 devices in a mesh: grp: 8 (over x, core), shard: 32 (over y, z).
Axes of the slice: x: 4, y: 4, z: 8, core: 2. Of those that a mesh axis runs over, the one named last changes fastest.
Arguments:
- inputs: bfloat16 [2, 1024, 4096], P(None, None, 'grp'), may hold values from -6 to 6
- up_cotangent: bfloat16 [2, 1024, 14336], P(None, None, 'shard'), may hold values from -0.1875 to 0.1875
- signs: int32 [4096, 16384], P('grp', 'shard'), may hold values from -1 to 1, as said below
- kept_row: int32 [8192], replicated, may hold values from 0 to 4095
- kept_col: int32 [8192], replicated, may hold values from 0 to 16383
Outputs:
- features: float32 [2, 8192], P(None, ('grp', 'shard'))
The draws below stay inside these ranges and needn't reach their ends.
Inputs may be any that keep to these rules, and one draw needn't show every extreme that they name: `signs`: every entry is -1 or +1.
All inputs are finite; a program needn't handle non-finite values.
Results may differ from the reference program's by a relative error of at most 0.0003.
Values sent between devices are 32-bit elements; how exact they have to be, the bound alone decides.
A program may use at most 320 MiB of HBM per device.

```python
import math
import jax
import jax.numpy as jnp

D = 4096
FF = 14336
FPAD = 16384
KEPT = 8192
S = 1024
EXAMPLES = 2
N_SHARD = 32


def draw_signs(key, part):
    key = jax.random.fold_in(key, 11)
    coins = jax.random.randint(key, (D, FPAD), 0, 2, dtype=jnp.int32)
    return 2 * coins - 1


def place_ends(entries, rng, least, largest):
    spot = [jax.random.randint(jax.random.fold_in(rng, axis), (), 0, length) for axis, length in enumerate(entries.shape)]
    main_axis = entries.shape.index(max(entries.shape))
    neighbour = spot[:main_axis] + [(spot[main_axis] + 1) % entries.shape[main_axis]] + spot[main_axis + 1:]
    return entries.at[tuple(spot)].set(least).at[tuple(neighbour)].set(largest)


def level_of(rng, dims, pieces, least, top_value):
    factor_of = 1.0
    for axis_at, shards_of in pieces:
        draws = jax.random.uniform(jax.random.fold_in(jax.random.fold_in(rng, 6), axis_at), (shards_of,), jnp.float32, least / len(pieces), top_value / len(pieces))
        factor_of = factor_of * jnp.repeat(jnp.exp(draws), dims[axis_at] // shards_of).reshape((-1,) + (1,) * (len(dims) - 1 - axis_at))
    return factor_of


def gaussian(own_key, extent, deviation, most, pieces=(), held_as=jnp.bfloat16):
    array = deviation * jax.random.normal(own_key, extent, jnp.float32)
    if pieces:
        array = array * level_of(own_key, extent, pieces, -0.22, 0.18)
    return jnp.clip(array, -most, most).astype(held_as)


def setup_inputs(seed: int = 0) -> dict:
    key_of = jax.random.split(jax.random.key(seed), 6)
    inputs = gaussian(key_of[0], (EXAMPLES, S, D), 1.0, 6.0, ((2, 8),))
    up_cotangent = gaussian(key_of[1], (EXAMPLES, S, FF), (S ** -0.5), 0.1875, ((2, 32),))
    signs = draw_signs(jax.random.fold_in(key_of[5], 71), 0)
    kept_row = place_ends(jax.random.randint(key_of[3], (KEPT,), 0, D), jax.random.fold_in(key_of[3], 1), 0, D - 1).astype(jnp.int32)
    kept_col = place_ends(jax.random.randint(key_of[4], (KEPT,), 0, FPAD), jax.random.fold_in(key_of[4], 1), 0, FPAD - 1).astype(jnp.int32)
    return {"inputs": inputs, "up_cotangent": up_cotangent, "signs": signs, "kept_row": kept_row, "kept_col": kept_col}


def walsh_transform(flat_values):
    length = flat_values.shape[0]
    half_width = 1
    while half_width < length:
        paired = flat_values.reshape(-1, 2, half_width)
        flat_values = jnp.stack([paired[:, 0] + paired[:, 1], paired[:, 0] - paired[:, 1]], axis=1).reshape(-1)
        half_width = half_width * 2
    return flat_values

def reference(inputs, up_cotangent, signs, kept_row, kept_col):
    results = []
    for example in range(EXAMPLES):
        gradient = jnp.dot(inputs[example].T, up_cotangent[example], preferred_element_type=jnp.float32)
        gradient = gradient.reshape(D, N_SHARD, FF // N_SHARD)
        gradient = jnp.pad(gradient, ((0, 0), (0, 0), (0, FPAD // N_SHARD - FF // N_SHARD)))
        placed = gradient.reshape(D, FPAD)
        signed = placed * signs.astype(jnp.float32)
        transformed = walsh_transform(signed.reshape(-1)).reshape(D, FPAD)
        results.append(transformed[kept_row, kept_col] / math.sqrt(D * FPAD))
    return jnp.stack(results)
```

```python
import math

import jax
import jax.numpy as jnp
from jax import lax
from jax.experimental import pallas as pl
from jax.experimental.pallas import tpu as pltpu
from jax.sharding import PartitionSpec as P

F32 = jnp.float32
BF16 = jnp.bfloat16
MESH = pl.DeviceIdType.MESH

EXAMPLES = 2
TOKENS = 1024
ROWS = 512
COLS = 512
UNITS = 448
KEPT = 8192
SCALE = 1.0 / math.sqrt(4096 * 16384)
GROUP = 16
NARROW = 64
PER_ROW = 16


def parity(bits):
    for shift in (8, 4, 2, 1):
        bits = bits ^ (bits >> shift)
    return bits & 1


def hadamard(shape):
    row = lax.broadcasted_iota(jnp.int32, shape, 0)
    col = lax.broadcasted_iota(jnp.int32, shape, 1)
    return jnp.where(parity(row & col) == 1, -1.0, 1.0).astype(BF16)


def lane_transform():
    row = lax.broadcasted_iota(jnp.int32, (256, 256), 0)
    col = lax.broadcasted_iota(jnp.int32, (256, 256), 1)
    target = ((col >> 7) << 6) | (col & 63)
    sign = jnp.where(parity((row & 127) & target) == 1, -1.0, 1.0)
    return jnp.where((row >> 7) == ((col >> 6) & 1), sign, 0.0).astype(BF16)


def split(values):
    high = values.astype(BF16)
    return high, (values - high.astype(F32)).astype(BF16)


def dot(a, b):
    return jnp.dot(a, b, preferred_element_type=F32)


def kernel(
    x_hbm, c_hbm, s_hbm, row_hbm, col_hbm, out_ref,
    x_ref, c_ref, s_ref, st_ref, row_ref, col_ref, lane_ref, q_vmem, q_smem, a_ref, table,
    send1, recv1, send2, recv2,
    sems, send1_sem, recv1_sem, send2_sem, recv2_sem,
):
    grp = lax.axis_index("grp")
    shard = lax.axis_index("shard")
    own1 = grp * 2 + shard // 16
    own2 = shard % 16

    def peer1(place):
        return (place // 2, (place % 2) * 16 + own2)

    def peer2(place):
        return (grp, (shard // 16) * 16 + place)

    copies = [
        pltpu.make_async_copy(row_hbm, row_ref, sems.at[0]),
        pltpu.make_async_copy(col_hbm, col_ref, sems.at[1]),
        pltpu.make_async_copy(s_hbm, s_ref, sems.at[2]),
        pltpu.make_async_copy(x_hbm.at[0], x_ref.at[0], sems.at[3]),
        pltpu.make_async_copy(c_hbm.at[0], c_ref.at[0], sems.at[4]),
        pltpu.make_async_copy(x_hbm.at[1], x_ref.at[1], sems.at[5]),
        pltpu.make_async_copy(c_hbm.at[1], c_ref.at[1], sems.at[6]),
    ]
    for copy in copies:
        copy.start()

    barrier = pltpu.get_barrier_semaphore()

    def greet(step, carry):
        pl.semaphore_signal(barrier, inc=1, device_id=peer1((own1 + 1 + step) % GROUP), device_id_type=MESH)
        pl.semaphore_signal(barrier, inc=1, device_id=peer2((own2 + 1 + step) % GROUP), device_id_type=MESH)
        return carry

    lax.fori_loop(0, GROUP - 1, greet, 0)

    h256 = hadamard((256, 256))
    lanes = lane_transform()

    copies[0].wait()
    copies[1].wait()
    row, col = row_ref[...], col_ref[...]
    q_vmem[...] = (((row & 511) >> 6) << 9) + (col & 511)
    q_copy = pltpu.make_async_copy(q_vmem, q_smem, sems.at[7])
    q_copy.start()
    device_bits = ((row >> 9) & grp) | (((col >> 9) & shard) << 3)
    lane_ref[...] = (row & (NARROW - 1)) | (parity(device_bits) << 7)

    copies[2].wait()
    st_ref[...] = jnp.transpose(s_ref[...].astype(F32))[:UNITS]
    low_table = jnp.concatenate([h256, h256], axis=1)
    high_table = jnp.concatenate([h256[:, : UNITS - 256], h256[:, : UNITS - 256]], axis=1)
    for e in range(EXAMPLES):
        copies[3 + 2 * e].wait()
        copies[4 + 2 * e].wait()
        for n in range(2):
            part = slice(256 * n, 256 * n + 256)
            signed = dot(c_ref[e], x_ref[e, :, part]) * st_ref[:, part]
            high, low = split(signed)
            first = dot(low_table, jnp.concatenate([high[:256], low[:256]], axis=0))
            second = dot(high_table, jnp.concatenate([high[256:], low[256:]], axis=0))
            a_ref[e, :256, part] = first + second
            a_ref[e, 256:, part] = first - second
    lanes2 = jnp.concatenate([lanes, lanes], axis=0)
    for j in range(4):
        part = slice(128 * j, 128 * j + 128)
        high, low = split(jnp.concatenate([a_ref[0, :, part], a_ref[1, :, part]], axis=1))
        both = dot(jnp.concatenate([high, low], axis=1), lanes2)
        table[pl.ds(2 * j * COLS, COLS)] = both[:, :128]
        table[pl.ds((2 * j + 1) * COLS, COLS)] = both[:, 128:]
    for p in range(2):
        t = [table[pl.ds((2 * j + p) * COLS, COLS)] for j in range(4)]
        a, b, c, d = t[0] + t[1], t[0] - t[1], t[2] + t[3], t[2] - t[3]
        for j, value in enumerate((a + c, b + d, a - c, b - d)):
            table[pl.ds((2 * j + p) * COLS, COLS)] = value
    q_copy.wait()

    lane = lax.broadcasted_iota(jnp.int32, (8, 128), 1)
    sublane = lax.broadcasted_iota(jnp.int32, (8, 128), 0)
    pattern = sublane * PER_ROW
    half = lane & NARROW
    place = lane & (NARROW - 1)

    def pick(block):
        def pair(step, carry):
            found, marks = carry
            for u in range(2):
                quarter = 2 * step + u
                r = 4 * block + quarter
                source = jnp.broadcast_to(lane_ref[pl.ds(r, 1), :], (8, 128))
                here = place - quarter * PER_ROW
                for m in range(PER_ROW):
                    rows = None
                    for i in range(8):
                        q = q_smem[r, i * PER_ROW + m]
                        one = jnp.broadcast_to(table[pl.ds(q, 1), :], (8, 128))
                        rows = one if rows is None else jnp.where(sublane == i, one, rows)
                    mark = jnp.take_along_axis(source, pattern + m, axis=1, mode="promise_in_bounds")
                    index = (mark & (NARROW - 1)) | half
                    got = jnp.take_along_axis(rows, index, axis=1, mode="promise_in_bounds")
                    found = jnp.where(here == m, got, found)
                    marks = jnp.where(here == m, mark, marks)
            return found, marks

        found, marks = lax.fori_loop(0, 2, pair, (jnp.zeros((8, 128), F32), jnp.zeros((8, 128), jnp.int32)))
        return found * jnp.where(marks >= 128, -SCALE, SCALE)

    def copy1(target, source):
        return pltpu.make_async_remote_copy(
            src_ref=send1.at[target], dst_ref=recv1.at[source], send_sem=send1_sem.at[target],
            recv_sem=recv1_sem.at[source], device_id=peer1(target), device_id_type=MESH,
        )

    def copy2(target, source):
        return pltpu.make_async_remote_copy(
            src_ref=send2.at[target % 4], dst_ref=recv2.at[source], send_sem=send2_sem.at[target],
            recv_sem=recv2_sem.at[source], device_id=peer2(target), device_id_type=MESH,
        )

    pl.semaphore_wait(barrier, 2 * (GROUP - 1))

    def produce(step, carry):
        target = (own1 + 1 + step) % GROUP
        send1[target] = pick(target)
        copy1(target, own1).start()
        return carry

    lax.fori_loop(0, GROUP - 1, produce, 0)
    total = pick(own1)

    def gather1(step, total):
        source = (own1 + GROUP - 1 - step) % GROUP
        copy1(source, source).wait_recv()
        return total + recv1[source]

    total = lax.fori_loop(0, GROUP - 1, gather1, total)
    for i in range(4):
        send2[i] = total[2 * i : 2 * i + 2]

    def spread(step, carry):
        copy2((own2 + 1 + step) % GROUP, own2).start()
        return carry

    lax.fori_loop(0, GROUP - 1, spread, 0)

    def gather2(step, total):
        source = (own2 + GROUP - 1 - step) % GROUP
        copy2(source, source).wait_recv()
        return total + recv2[source]

    total = lax.fori_loop(0, GROUP - 1, gather2, send2[own2 % 4])
    quarter = (shard // 4) % 4
    total = pltpu.roll(total, (128 - quarter * PER_ROW) % 128, 1)
    for e in range(EXAMPLES):
        for i in range(2):
            out_ref[e : e + 1, PER_ROW * i : PER_ROW * i + PER_ROW] = total[i : i + 1, NARROW * e : NARROW * e + PER_ROW]

    def finish(step, carry):
        copy1((own1 + 1 + step) % GROUP, own1).wait_send()
        copy2((own2 + 1 + step) % GROUP, own2).wait_send()
        return carry

    lax.fori_loop(0, GROUP - 1, finish, 0)


def local(inputs, up_cotangent, signs, kept_row, kept_col):
    hbm = pl.BlockSpec(memory_space=pl.ANY)
    return pl.pallas_call(
        kernel,
        out_shape=jax.ShapeDtypeStruct((EXAMPLES, KEPT // 256), F32),
        in_specs=[hbm] * 5,
        out_specs=pl.BlockSpec(memory_space=pltpu.VMEM),
        scratch_shapes=[
            pltpu.VMEM((EXAMPLES, TOKENS, ROWS), BF16),
            pltpu.VMEM((EXAMPLES, UNITS, TOKENS), BF16),
            pltpu.VMEM((ROWS, COLS), jnp.int32),
            pltpu.VMEM((UNITS, ROWS), F32),
            pltpu.VMEM((64, 128), jnp.int32),
            pltpu.VMEM((64, 128), jnp.int32),
            pltpu.VMEM((64, 128), jnp.int32),
            pltpu.VMEM((64, 128), jnp.int32),
            pltpu.SMEM((64, 128), jnp.int32),
            pltpu.VMEM((EXAMPLES, COLS, ROWS), F32),
            pltpu.VMEM((8 * COLS, 128), F32),
            pltpu.VMEM((GROUP, 8, 128), F32),
            pltpu.VMEM((GROUP, 8, 128), F32),
            pltpu.VMEM((4, 2, 128), F32),
            pltpu.VMEM((GROUP, 2, 128), F32),
            pltpu.SemaphoreType.DMA((8,)),
            pltpu.SemaphoreType.DMA((GROUP,)),
            pltpu.SemaphoreType.DMA((GROUP,)),
            pltpu.SemaphoreType.DMA((GROUP,)),
            pltpu.SemaphoreType.DMA((GROUP,)),
        ],
        compiler_params=pltpu.CompilerParams(
            vmem_limit_bytes=60 << 20, collective_id=0, has_side_effects=True
        ),
    )(inputs, jnp.swapaxes(up_cotangent, 1, 2), signs, kept_row.reshape(64, 128), kept_col.reshape(64, 128))


def solution(mesh):
    placed = (P(None, None, "grp"), P(None, None, "shard"), P("grp", "shard"), P(), P())
    return jax.shard_map(
        local, mesh=mesh, in_specs=placed, out_specs=P(None, ("grp", "shard")), check_vma=False
    )
```

```python
import math

import jax
import jax.numpy as jnp
from jax import lax
from jax.experimental import pallas as pl
from jax.experimental.pallas import tpu as pltpu
from jax.sharding import PartitionSpec as P

F32 = jnp.float32
BF16 = jnp.bfloat16
MESH = pl.DeviceIdType.MESH

EXAMPLES = 2
TOKENS = 1024
ROWS = 512
COLS = 512
UNITS = 448
KEPT = 8192
SCALE = 1.0 / math.sqrt(4096 * 16384)
GROUP = 16
NARROW = 64
PER_ROW = 16


def parity(bits):
    for shift in (8, 4, 2, 1):
        bits = bits ^ (bits >> shift)
    return bits & 1


def hadamard(shape):
    row = lax.broadcasted_iota(jnp.int32, shape, 0)
    col = lax.broadcasted_iota(jnp.int32, shape, 1)
    return jnp.where(parity(row & col) == 1, -1.0, 1.0).astype(BF16)


def lane_transform():
    row = lax.broadcasted_iota(jnp.int32, (256, 256), 0)
    col = lax.broadcasted_iota(jnp.int32, (256, 256), 1)
    target = ((col >> 7) << 6) | (col & 63)
    sign = jnp.where(parity((row & 127) & target) == 1, -1.0, 1.0)
    return jnp.where((row >> 7) == ((col >> 6) & 1), sign, 0.0).astype(BF16)


def split(values):
    high = values.astype(BF16)
    return high, (values - high.astype(F32)).astype(BF16)


def permute(values, index):
    numbers = lax.GatherDimensionNumbers(
        offset_dims=(), collapsed_slice_dims=(1,), start_index_map=(1,),
        operand_batching_dims=(0,), start_indices_batching_dims=(0,),
    )
    return lax.gather(values, index[..., None], numbers, (1, 1), mode=lax.GatherScatterMode.PROMISE_IN_BOUNDS)


def spread_table(columns, chosen):
    row = lax.broadcasted_iota(jnp.int32, (128, columns), 0)
    col = lax.broadcasted_iota(jnp.int32, (128, columns), 1)
    return jnp.where((row & (PER_ROW - 1)) == chosen(col), 1.0, 0.0).astype(BF16)


def dot(a, b):
    return jnp.dot(a, b, preferred_element_type=F32)


def kernel(
    x_hbm, c_hbm, s_hbm, row_hbm, col_hbm, out_ref,
    x_ref, c_ref, s_ref, st_ref, row_ref, col_ref, q_vmem, q_smem, index_ref, sign_ref, split_ref, table,
    send1, recv1, send2, recv2,
    sems, send1_sem, recv1_sem, send2_sem, recv2_sem,
):
    grp = lax.axis_index("grp")
    shard = lax.axis_index("shard")
    own1 = grp * 2 + shard // 16
    own2 = shard % 16

    def peer1(place):
        return (place // 2, (place % 2) * 16 + own2)

    def peer2(place):
        return (grp, (shard // 16) * 16 + place)

    copies = [
        pltpu.make_async_copy(row_hbm, row_ref, sems.at[0]),
        pltpu.make_async_copy(col_hbm, col_ref, sems.at[1]),
        pltpu.make_async_copy(s_hbm, s_ref, sems.at[2]),
        pltpu.make_async_copy(x_hbm.at[0], x_ref.at[0], sems.at[3]),
        pltpu.make_async_copy(c_hbm.at[0], c_ref.at[0], sems.at[4]),
        pltpu.make_async_copy(x_hbm.at[1], x_ref.at[1], sems.at[5]),
        pltpu.make_async_copy(c_hbm.at[1], c_ref.at[1], sems.at[6]),
    ]
    for copy in copies:
        copy.start()

    barrier = pltpu.get_barrier_semaphore()

    def greet(step, carry):
        pl.semaphore_signal(barrier, inc=1, device_id=peer1((own1 + 1 + step) % GROUP), device_id_type=MESH)
        pl.semaphore_signal(barrier, inc=1, device_id=peer2((own2 + 1 + step) % GROUP), device_id_type=MESH)
        return carry

    lax.fori_loop(0, GROUP - 1, greet, 0)

    h256 = hadamard((256, 256))
    lanes = lane_transform()

    copies[0].wait()
    copies[1].wait()
    row, col = row_ref[...], col_ref[...]
    q_vmem[...] = (((row & 511) >> 6) << 9) + (col & 511)
    q_copy = pltpu.make_async_copy(q_vmem, q_smem, sems.at[7])
    q_copy.start()
    lane = lax.broadcasted_iota(jnp.int32, (8, 128), 1)
    sublane = lax.broadcasted_iota(jnp.int32, (8, 128), 0)
    device_bits = ((row >> 9) & grp) | (((col >> 9) & shard) << 3)
    sign = jnp.where(parity(device_bits) == 1, -1.0, 1.0)
    inner = (row & (NARROW - 1)).astype(F32)
    mine = (lane // PER_ROW) == sublane

    def diagonal(values):
        blocks = [jnp.where(mine, jnp.broadcast_to(values[r : r + 1], (8, 128)), 0.0) for r in range(64)]
        return jnp.concatenate(blocks, axis=0).astype(BF16)

    spots = diagonal(inner)
    for pair in range(PER_ROW // 2):
        found = dot(spots, spread_table(256, lambda y: 2 * pair + (y >> 7))).astype(jnp.int32)
        for u in range(2):
            part = found[:, 128 * u : 128 * u + 128].reshape(64, 8, 128)
            index_ref[:, 2 * pair + u] = part + (lane & NARROW)[None]
    found = dot(diagonal(sign), spread_table(128, lambda y: y & (PER_ROW - 1))) * SCALE
    for b in range(GROUP):
        value = found[32 * b : 32 * b + 8]
        for quarter in range(1, 4):
            here = ((lane // PER_ROW) & 3) == quarter
            value = jnp.where(here, found[32 * b + 8 * quarter : 32 * b + 8 * quarter + 8], value)
        sign_ref[b] = value

    copies[2].wait()
    st_ref[...] = jnp.transpose(s_ref[...].astype(F32))[:UNITS]
    low_table = jnp.concatenate([h256, h256], axis=1)
    high_table = jnp.concatenate([h256[:, : UNITS - 256], h256[:, : UNITS - 256]], axis=1)
    for e in range(EXAMPLES):
        copies[3 + 2 * e].wait()
        copies[4 + 2 * e].wait()
        signed = dot(c_ref[e], x_ref[e]) * st_ref[...]
        t = [signed[:, 128 * j : 128 * j + 128] for j in range(4)]
        a, b, c, d = t[0] + t[1], t[0] - t[1], t[2] + t[3], t[2] - t[3]
        part = slice(128 * e, 128 * e + 128)
        for j, value in enumerate((a + c, b + d, a - c, b - d)):
            high, low = split(value)
            split_ref[j, :256, part] = high[:256]
            split_ref[j, 256:512, part] = low[:256]
            split_ref[j, 512 : 256 + UNITS, part] = high[256:]
            split_ref[j, 256 + UNITS :, part] = low[256:]
    lanes2 = jnp.concatenate([lanes, lanes], axis=0)
    for j in range(4):
        first = dot(low_table, split_ref[j, :512])
        second = dot(high_table, split_ref[j, 512:])
        for upper, value in enumerate((first + second, first - second)):
            high, low = split(value)
            both = dot(jnp.concatenate([high, low], axis=1), lanes2)
            table[pl.ds(2 * j * COLS + 256 * upper, 256)] = both[:, :128]
            table[pl.ds((2 * j + 1) * COLS + 256 * upper, 256)] = both[:, 128:]
    q_copy.wait()

    place = lane & (NARROW - 1)

    def pick(block):
        found = jnp.zeros((8, 128), F32)
        for quarter in range(4):
            r = 4 * block + quarter
            for m in range(PER_ROW):
                rows = None
                for i in range(8):
                    q = q_smem.at[:, pl.ds(i * PER_ROW + m, 1)][r, 0]
                    one = jnp.broadcast_to(table[pl.ds(q, 1), :], (8, 128))
                    rows = one if rows is None else jnp.where(sublane == i, one, rows)
                found = jnp.where(place == quarter * PER_ROW + m, permute(rows, index_ref[r, m]), found)
        return found * sign_ref[block]

    def copy1(target, source):
        return pltpu.make_async_remote_copy(
            src_ref=send1.at[target], dst_ref=recv1.at[source], send_sem=send1_sem.at[target],
            recv_sem=recv1_sem.at[source], device_id=peer1(target), device_id_type=MESH,
        )

    def copy2(target, source):
        return pltpu.make_async_remote_copy(
            src_ref=send2.at[target % 4], dst_ref=recv2.at[source], send_sem=send2_sem.at[target],
            recv_sem=recv2_sem.at[source], device_id=peer2(target), device_id_type=MESH,
        )

    pl.semaphore_wait(barrier, 2 * (GROUP - 1))

    def produce(step, carry):
        target = (own1 + 1 + step) % GROUP
        send1[target] = pick(target)

        @pl.when(step < GROUP - 1)
        def _():
            copy1(target, own1).start()

        return carry

    lax.fori_loop(0, GROUP, produce, 0)

    def gather1(step, total):
        source = (own1 + GROUP - 1 - step) % GROUP
        copy1(source, source).wait_recv()
        return total + recv1[source]

    total = lax.fori_loop(0, GROUP - 1, gather1, send1[own1])
    for i in range(4):
        send2[i] = total[2 * i : 2 * i + 2]

    def spread(step, carry):
        copy2((own2 + 1 + step) % GROUP, own2).start()
        return carry

    lax.fori_loop(0, GROUP - 1, spread, 0)

    def gather2(step, total):
        source = (own2 + GROUP - 1 - step) % GROUP
        copy2(source, source).wait_recv()
        return total + recv2[source]

    total = lax.fori_loop(0, GROUP - 1, gather2, send2[own2 % 4])
    quarter = (shard // 4) % 4
    total = pltpu.roll(total, (128 - quarter * PER_ROW) % 128, 1)
    for e in range(EXAMPLES):
        for i in range(2):
            out_ref[e : e + 1, PER_ROW * i : PER_ROW * i + PER_ROW] = total[i : i + 1, NARROW * e : NARROW * e + PER_ROW]

    def finish(step, carry):
        copy1((own1 + 1 + step) % GROUP, own1).wait_send()
        copy2((own2 + 1 + step) % GROUP, own2).wait_send()
        return carry

    lax.fori_loop(0, GROUP - 1, finish, 0)


def local(inputs, up_cotangent, signs, kept_row, kept_col):
    hbm = pl.BlockSpec(memory_space=pl.ANY)
    return pl.pallas_call(
        kernel,
        out_shape=jax.ShapeDtypeStruct((EXAMPLES, KEPT // 256), F32),
        in_specs=[hbm] * 5,
        out_specs=pl.BlockSpec(memory_space=pltpu.VMEM),
        scratch_shapes=[
            pltpu.VMEM((EXAMPLES, TOKENS, ROWS), BF16),
            pltpu.VMEM((EXAMPLES, UNITS, TOKENS), BF16),
            pltpu.VMEM((ROWS, COLS), jnp.int32),
            pltpu.VMEM((UNITS, ROWS), F32),
            pltpu.VMEM((64, 128), jnp.int32),
            pltpu.VMEM((64, 128), jnp.int32),
            pltpu.VMEM((64, 128), jnp.int32),
            pltpu.SMEM((64, 128), jnp.int32),
            pltpu.VMEM((64, PER_ROW, 8, 128), jnp.int32),
            pltpu.VMEM((GROUP, 8, 128), F32),
            pltpu.VMEM((4, 2 * UNITS, 256), BF16),
            pltpu.VMEM((8 * COLS, 128), F32),
            pltpu.VMEM((GROUP, 8, 128), F32),
            pltpu.VMEM((GROUP, 8, 128), F32),
            pltpu.VMEM((4, 2, 128), F32),
            pltpu.VMEM((GROUP, 2, 128), F32),
            pltpu.SemaphoreType.DMA((8,)),
            pltpu.SemaphoreType.DMA((GROUP,)),
            pltpu.SemaphoreType.DMA((GROUP,)),
            pltpu.SemaphoreType.DMA((GROUP,)),
            pltpu.SemaphoreType.DMA((GROUP,)),
        ],
        compiler_params=pltpu.CompilerParams(
            vmem_limit_bytes=64 << 20, collective_id=0, has_side_effects=True
        ),
    )(inputs, jnp.swapaxes(up_cotangent, 1, 2), signs, kept_row.reshape(64, 128), kept_col.reshape(64, 128))


def solution(mesh):
    placed = (P(None, None, "grp"), P(None, None, "shard"), P("grp", "shard"), P(), P())
    return jax.shard_map(
        local, mesh=mesh, in_specs=placed, out_specs=P(None, ("grp", "shard")), check_vma=False
    )
```

```python
import math

import jax
import jax.numpy as jnp
from jax import lax
from jax.experimental import pallas as pl
from jax.experimental.pallas import tpu as pltpu
from jax.sharding import PartitionSpec as P

F32 = jnp.float32
BF16 = jnp.bfloat16
MESH = pl.DeviceIdType.MESH

EXAMPLES = 2
TOKENS = 1024
ROWS = 512
COLS = 512
UNITS = 448
KEPT = 8192
SCALE = 1.0 / math.sqrt(4096 * 16384)
FIRST = 32
SECOND = 8
NARROW = 64
PER_ROW = 16


def parity(bits):
    for shift in (8, 4, 2, 1):
        bits = bits ^ (bits >> shift)
    return bits & 1


def hadamard(shape):
    row = lax.broadcasted_iota(jnp.int32, shape, 0)
    col = lax.broadcasted_iota(jnp.int32, shape, 1)
    return jnp.where(parity(row & col) == 1, -1.0, 1.0).astype(BF16)


def lane_transform():
    row = lax.broadcasted_iota(jnp.int32, (256, 256), 0)
    col = lax.broadcasted_iota(jnp.int32, (256, 256), 1)
    target = ((col >> 7) << 6) | (col & 63)
    sign = jnp.where(parity((row & 127) & target) == 1, -1.0, 1.0)
    return jnp.where((row >> 7) == ((col >> 6) & 1), sign, 0.0).astype(BF16)


def split(values):
    high = values.astype(BF16)
    return high, (values - high.astype(F32)).astype(BF16)


def permute(values, index):
    numbers = lax.GatherDimensionNumbers(
        offset_dims=(), collapsed_slice_dims=(1,), start_index_map=(1,),
        operand_batching_dims=(0,), start_indices_batching_dims=(0,),
    )
    return lax.gather(values, index[..., None], numbers, (1, 1), mode=lax.GatherScatterMode.PROMISE_IN_BOUNDS)


def spread_table(columns, chosen):
    row = lax.broadcasted_iota(jnp.int32, (128, columns), 0)
    col = lax.broadcasted_iota(jnp.int32, (128, columns), 1)
    return jnp.where((row & (PER_ROW - 1)) == chosen(col), 1.0, 0.0).astype(BF16)


def dot(a, b):
    return jnp.dot(a, b, preferred_element_type=F32)


def hops(offset, length):
    return min(offset, length - offset)


def pack(order, width):
    words = [sum(order[6 * w + n] << (width * n) for n in range(6) if 6 * w + n < len(order)) for w in range((len(order) + 5) // 6)]

    def read(step):
        word = words[-1]
        for w in range(len(words) - 2, -1, -1):
            word = jnp.where(step // 6 == w, words[w], word)
        return (word >> (width * (step % 6))) & ((1 << width) - 1)

    return read


first_order = sorted(range(FIRST), key=lambda c: -hops(c // 8, 4) - hops(c % 8, 8))
second_order = sorted(range(SECOND), key=lambda c: (-hops(c // 2, 4), -(c % 2)))
first_offset = pack(first_order, 5)
second_offset = pack(second_order, 3)


def kernel(
    x_hbm, c_hbm, s_hbm, row_hbm, col_hbm, out_ref,
    x_ref, c_ref, s_ref, st_ref, row_ref, col_ref, q_vmem, q_smem, index_ref, sign_ref, split_ref, table,
    send1, recv1, send2, recv2,
    sems, send1_sem, recv1_sem, send2_sem, recv2_sem,
):
    grp = lax.axis_index("grp")
    shard = lax.axis_index("shard")

    def peer1(step, sign):
        code = first_offset(step)
        y = (shard // 8 + 4 + sign * (code // 8)) % 4
        z = (shard % 8 + 8 + sign * (code % 8)) % 8
        return y * 8 + z

    def peer2(step, sign):
        code = second_offset(step)
        x = (grp // 2 + 4 + sign * (code // 2)) % 4
        return x * 2 + (grp + code) % 2

    copies = [
        pltpu.make_async_copy(row_hbm, row_ref, sems.at[0]),
        pltpu.make_async_copy(col_hbm, col_ref, sems.at[1]),
        pltpu.make_async_copy(s_hbm, s_ref, sems.at[2]),
        pltpu.make_async_copy(x_hbm.at[0], x_ref.at[0], sems.at[3]),
        pltpu.make_async_copy(c_hbm.at[0], c_ref.at[0], sems.at[4]),
        pltpu.make_async_copy(x_hbm.at[1], x_ref.at[1], sems.at[5]),
        pltpu.make_async_copy(c_hbm.at[1], c_ref.at[1], sems.at[6]),
    ]
    for copy in copies:
        copy.start()

    barrier = pltpu.get_barrier_semaphore()

    def greet1(step, carry):
        pl.semaphore_signal(barrier, inc=1, device_id=(grp, peer1(step, -1)), device_id_type=MESH)
        return carry

    def greet2(step, carry):
        pl.semaphore_signal(barrier, inc=1, device_id=(peer2(step, -1), shard), device_id_type=MESH)
        return carry

    lax.fori_loop(0, FIRST - 1, greet1, 0)
    lax.fori_loop(0, SECOND - 1, greet2, 0)

    h256 = hadamard((256, 256))
    lanes = lane_transform()

    copies[0].wait()
    copies[1].wait()
    row, col = row_ref[...], col_ref[...]
    device_bits = ((row >> 9) & grp) | (((col >> 9) & shard) << 3)
    entry = ((row & 511) >> 6) * COLS + (col & 511)
    packed = entry | ((row & (NARROW - 1)) << 12) | (parity(device_bits) << 18)
    lane = lax.broadcasted_iota(jnp.int32, (8, 128), 1)
    sublane = lax.broadcasted_iota(jnp.int32, (8, 128), 0)
    ordered = []
    for chunk in range(8):
        at = (chunk % 4) * 2 + chunk // 4
        value = None
        for i in range(SECOND):
            moved = packed[8 * i : 8 * i + 8]
            if i != at:
                moved = pltpu.roll(moved, ((i - at) % 8) * PER_ROW, 1)
            value = moved if value is None else jnp.where(lane // PER_ROW == i, moved, value)
        ordered.append(value)
    packed = jnp.concatenate(ordered, axis=0)
    q_vmem[...] = packed & 4095
    q_copy = pltpu.make_async_copy(q_vmem, q_smem, sems.at[7])
    q_copy.start()
    sign = jnp.where((packed >> 18) == 1, -1.0, 1.0)
    inner = ((packed >> 12) & (NARROW - 1)).astype(F32)
    mine = (lane // PER_ROW) == sublane

    def diagonal(values):
        blocks = [jnp.where(mine, jnp.broadcast_to(values[r : r + 1], (8, 128)), 0.0) for r in range(64)]
        return jnp.concatenate(blocks, axis=0).astype(BF16)

    spots = diagonal(inner)
    for pair in range(PER_ROW // 2):
        found = dot(spots, spread_table(256, lambda y: 2 * pair + (y >> 7))).astype(jnp.int32)
        for u in range(2):
            part = found[:, 128 * u : 128 * u + 128].reshape(64, 8, 128)
            index_ref[:, 2 * pair + u] = part + (lane & NARROW)[None]
    found = dot(diagonal(sign), spread_table(128, lambda y: y & (PER_ROW - 1))) * SCALE
    for r in range(FIRST):
        second_half = found[8 * (FIRST + r) : 8 * (FIRST + r) + 8]
        sign_ref[r] = jnp.where((lane // PER_ROW) % 2 == 1, second_half, found[8 * r : 8 * r + 8])

    copies[2].wait()
    st_ref[...] = jnp.transpose(s_ref[...].astype(F32))[:UNITS]
    low_table = jnp.concatenate([h256, h256], axis=1)
    high_table = jnp.concatenate([h256[:, : UNITS - 256], h256[:, : UNITS - 256]], axis=1)
    for e in range(EXAMPLES):
        copies[3 + 2 * e].wait()
        copies[4 + 2 * e].wait()
        signed = dot(c_ref[e], x_ref[e]) * st_ref[...]
        t = [signed[:, 128 * j : 128 * j + 128] for j in range(4)]
        a, b, c, d = t[0] + t[1], t[0] - t[1], t[2] + t[3], t[2] - t[3]
        part = slice(128 * e, 128 * e + 128)
        for j, value in enumerate((a + c, b + d, a - c, b - d)):
            high, low = split(value)
            split_ref[j, :256, part] = high[:256]
            split_ref[j, 256:512, part] = low[:256]
            split_ref[j, 512 : 256 + UNITS, part] = high[256:]
            split_ref[j, 256 + UNITS :, part] = low[256:]
    lanes2 = jnp.concatenate([lanes, lanes], axis=0)
    for j in range(4):
        first = dot(low_table, split_ref[j, :512])
        second = dot(high_table, split_ref[j, 512:])
        for upper, value in enumerate((first + second, first - second)):
            high, low = split(value)
            both = dot(jnp.concatenate([high, low], axis=1), lanes2)
            table[pl.ds(2 * j * COLS + 256 * upper, 256)] = both[:, :128]
            table[pl.ds((2 * j + 1) * COLS + 256 * upper, 256)] = both[:, 128:]
    q_copy.wait()

    place = lane & (NARROW - 1)

    def pick(target):
        block = (target % 4) * 8 + target // 4
        found = jnp.zeros((8, 128), F32)
        for half in range(2):
            r = block + half * FIRST
            for m in range(PER_ROW):
                rows = None
                for i in range(SECOND):
                    q = q_smem.at[:, pl.ds(i * PER_ROW + m, 1)][r, 0]
                    one = jnp.broadcast_to(table[pl.ds(q, 1), :], (8, 128))
                    rows = one if rows is None else jnp.where(sublane == i, one, rows)
                found = jnp.where(place == half * PER_ROW + m, permute(rows, index_ref[r, m]), found)
        return found * sign_ref[block]

    pl.semaphore_wait(barrier, FIRST + SECOND - 2)

    def produce(step, carry):
        target = peer1(step, 1)
        send1[step] = pick(target)

        @pl.when(step < FIRST - 1)
        def _():
            pltpu.make_async_remote_copy(
                src_ref=send1.at[step], dst_ref=recv1.at[step], send_sem=send1_sem, recv_sem=recv1_sem,
                device_id=(grp, target), device_id_type=MESH,
            ).start()

        return carry

    lax.fori_loop(0, FIRST, produce, 0)
    pltpu.make_async_copy(recv1, recv1, recv1_sem).wait()
    total = send1[FIRST - 1]
    for step in range(FIRST - 1):
        total = total + recv1[step]
    for g in range(SECOND):
        send2[g] = total[g : g + 1]
    for step in range(SECOND - 1):
        target = peer2(step, 1)
        pltpu.make_async_remote_copy(
            src_ref=send2.at[target], dst_ref=recv2.at[step], send_sem=send2_sem, recv_sem=recv2_sem,
            device_id=(target, shard), device_id_type=MESH,
        ).start()
    sent = send1.at[pl.ds(0, FIRST - 1)]
    pltpu.make_async_copy(sent, sent, send1_sem).wait()
    total = send2[grp]
    pltpu.make_async_copy(recv2, recv2, recv2_sem).wait()
    for step in range(SECOND - 1):
        total = total + recv2[step]
    for e in range(EXAMPLES):
        out_ref[e : e + 1, :] = total[:, NARROW * e : NARROW * e + KEPT // 256]
    pltpu.make_async_copy(recv2, recv2, send2_sem).wait()


def local(inputs, up_cotangent, signs, kept_row, kept_col):
    hbm = pl.BlockSpec(memory_space=pl.ANY)
    return pl.pallas_call(
        kernel,
        out_shape=jax.ShapeDtypeStruct((EXAMPLES, KEPT // 256), F32),
        in_specs=[hbm] * 5,
        out_specs=pl.BlockSpec(memory_space=pltpu.VMEM),
        scratch_shapes=[
            pltpu.VMEM((EXAMPLES, TOKENS, ROWS), BF16),
            pltpu.VMEM((EXAMPLES, UNITS, TOKENS), BF16),
            pltpu.VMEM((ROWS, COLS), jnp.int32),
            pltpu.VMEM((UNITS, ROWS), F32),
            pltpu.VMEM((64, 128), jnp.int32),
            pltpu.VMEM((64, 128), jnp.int32),
            pltpu.VMEM((64, 128), jnp.int32),
            pltpu.SMEM((64, 128), jnp.int32),
            pltpu.VMEM((64, PER_ROW, 8, 128), jnp.int32),
            pltpu.VMEM((FIRST, 8, 128), F32),
            pltpu.VMEM((4, 2 * UNITS, 256), BF16),
            pltpu.VMEM((8 * COLS, 128), F32),
            pltpu.VMEM((FIRST, 8, 128), F32),
            pltpu.VMEM((FIRST - 1, 8, 128), F32),
            pltpu.VMEM((SECOND, 1, 128), F32),
            pltpu.VMEM((SECOND - 1, 1, 128), F32),
            pltpu.SemaphoreType.DMA((8,)),
            pltpu.SemaphoreType.DMA,
            pltpu.SemaphoreType.DMA,
            pltpu.SemaphoreType.DMA,
            pltpu.SemaphoreType.DMA,
        ],
        compiler_params=pltpu.CompilerParams(
            vmem_limit_bytes=64 << 20, collective_id=0, has_side_effects=True
        ),
    )(inputs, jnp.swapaxes(up_cotangent, 1, 2), signs, kept_row.reshape(64, 128), kept_col.reshape(64, 128))


def solution(mesh):
    placed = (P(None, None, "grp"), P(None, None, "shard"), P("grp", "shard"), P(), P())
    return jax.shard_map(
        local, mesh=mesh, in_specs=placed, out_specs=P(None, ("grp", "shard")), check_vma=False
    )
```

```python
import math

import jax
import jax.numpy as jnp
from jax import lax
from jax.experimental import pallas as pl
from jax.experimental.pallas import tpu as pltpu
from jax.sharding import PartitionSpec as P

F32 = jnp.float32
BF16 = jnp.bfloat16
MESH = pl.DeviceIdType.MESH

EXAMPLES = 2
TOKENS = 1024
ROWS = 512
COLS = 512
UNITS = 448
KEPT = 8192
SCALE = 1.0 / math.sqrt(4096 * 16384)
FIRST = 32
SECOND = 8
NARROW = 64
PER_ROW = 16


def parity(bits):
    for shift in (8, 4, 2, 1):
        bits = bits ^ (bits >> shift)
    return bits & 1


def hadamard(shape):
    row = lax.broadcasted_iota(jnp.int32, shape, 0)
    col = lax.broadcasted_iota(jnp.int32, shape, 1)
    return jnp.where(parity(row & col) == 1, -1.0, 1.0).astype(BF16)


def lane_transform():
    row = lax.broadcasted_iota(jnp.int32, (256, 256), 0)
    col = lax.broadcasted_iota(jnp.int32, (256, 256), 1)
    target = ((col >> 7) << 6) | (col & 63)
    sign = jnp.where(parity((row & 127) & target) == 1, -1.0, 1.0)
    return jnp.where((row >> 7) == ((col >> 6) & 1), sign, 0.0).astype(BF16)


def split(values):
    high = values.astype(BF16)
    return high, (values - high.astype(F32)).astype(BF16)


def permute(values, index):
    numbers = lax.GatherDimensionNumbers(
        offset_dims=(), collapsed_slice_dims=(1,), start_index_map=(1,),
        operand_batching_dims=(0,), start_indices_batching_dims=(0,),
    )
    return lax.gather(values, index[..., None], numbers, (1, 1), mode=lax.GatherScatterMode.PROMISE_IN_BOUNDS)


def spread_table(columns, chosen):
    row = lax.broadcasted_iota(jnp.int32, (128, columns), 0)
    col = lax.broadcasted_iota(jnp.int32, (128, columns), 1)
    return jnp.where((row & (PER_ROW - 1)) == chosen(col), 1.0, 0.0).astype(BF16)


def dot(a, b):
    return jnp.dot(a, b, preferred_element_type=F32)


def hops(offset, length):
    return min(offset, length - offset)


def pack(order):
    words = [sum(code << (8 * n) for n, code in enumerate(order[w : w + 4])) for w in range(0, len(order), 4)]

    def read(step):
        word = words[-1]
        for w in range(len(words) - 2, -1, -1):
            word = jnp.where((step >> 2) == w, words[w], word)
        return (word >> ((step & 3) * 8)) & 31

    return read


first_order = sorted(range(FIRST), key=lambda c: -hops(c // 8, 4) - hops(c % 8, 8))
second_order = sorted(range(SECOND), key=lambda c: (-hops(c // 2, 4), -(c % 2)))
first_offset = pack(first_order)


def kernel(
    x_hbm, c_hbm, s_hbm, row_hbm, col_hbm, out_ref,
    x_ref, c_ref, s_ref, st_ref, row_ref, col_ref, q_vmem, q_smem, index_ref, sign_ref, split_ref, table,
    send1, recv1, send2, recv2,
    sems, send1_sem, recv1_sem, send2_sem, recv2_sem,
):
    grp = lax.axis_index("grp")
    shard = lax.axis_index("shard")

    def peer1(step):
        code = first_offset(step)
        return ((shard + (code & 24)) & 24) | ((shard + code) & 7)

    def peer2(step):
        code = second_order[step]
        return ((grp + (code & 6)) & 6) | ((grp ^ code) & 1)

    copies = [
        pltpu.make_async_copy(row_hbm, row_ref, sems.at[0]),
        pltpu.make_async_copy(col_hbm, col_ref, sems.at[1]),
        pltpu.make_async_copy(s_hbm, s_ref, sems.at[2]),
        pltpu.make_async_copy(x_hbm.at[0], x_ref.at[0], sems.at[3]),
        pltpu.make_async_copy(c_hbm.at[0], c_ref.at[0], sems.at[4]),
        pltpu.make_async_copy(x_hbm.at[1], x_ref.at[1], sems.at[5]),
        pltpu.make_async_copy(c_hbm.at[1], c_ref.at[1], sems.at[6]),
    ]
    for copy in copies:
        copy.start()

    barrier = pltpu.get_barrier_semaphore()

    def greet(step, carry):
        pl.semaphore_signal(barrier, inc=1, device_id=(grp, shard ^ step), device_id_type=MESH)
        return carry

    lax.fori_loop(1, FIRST, greet, 0)
    for step in range(1, SECOND):
        pl.semaphore_signal(barrier, inc=1, device_id=(grp ^ step, shard), device_id_type=MESH)

    h256 = hadamard((256, 256))
    lanes = lane_transform()

    copies[0].wait()
    copies[1].wait()
    row, col = row_ref[...], col_ref[...]
    device_bits = ((row >> 9) & grp) | (((col >> 9) & shard) << 3)
    entry = ((row & 511) >> 6) * COLS + (col & 511)
    packed = entry | ((row & (NARROW - 1)) << 12) | (parity(device_bits) << 18)
    lane = lax.broadcasted_iota(jnp.int32, (8, 128), 1)
    sublane = lax.broadcasted_iota(jnp.int32, (8, 128), 0)
    ordered = []
    for chunk in range(8):
        at = (chunk % 4) * 2 + chunk // 4
        value = None
        for i in range(SECOND):
            moved = packed[8 * i : 8 * i + 8]
            if i != at:
                moved = pltpu.roll(moved, ((i - at) % 8) * PER_ROW, 1)
            value = moved if value is None else jnp.where(lane // PER_ROW == i, moved, value)
        ordered.append(value)
    packed = jnp.concatenate(ordered, axis=0)
    q_vmem[...] = packed & 4095
    q_copy = pltpu.make_async_copy(q_vmem, q_smem, sems.at[7])
    q_copy.start()
    sign = jnp.where((packed >> 18) == 1, -1.0, 1.0)
    inner = ((packed >> 12) & (NARROW - 1)).astype(F32)
    mine = (lane // PER_ROW) == sublane

    def diagonal(values):
        blocks = [jnp.where(mine, jnp.broadcast_to(values[r : r + 1], (8, 128)), 0.0) for r in range(64)]
        return jnp.concatenate(blocks, axis=0).astype(BF16)

    spots = diagonal(inner)
    for pair in range(PER_ROW // 2):
        found = dot(spots, spread_table(256, lambda y: 2 * pair + (y >> 7))).astype(jnp.int32)
        for u in range(2):
            part = found[:, 128 * u : 128 * u + 128].reshape(64, 8, 128)
            index_ref[:, 2 * pair + u] = part + (lane & NARROW)[None]
    found = dot(diagonal(sign), spread_table(128, lambda y: y & (PER_ROW - 1))) * SCALE
    for r in range(FIRST):
        second_half = found[8 * (FIRST + r) : 8 * (FIRST + r) + 8]
        sign_ref[r] = jnp.where((lane // PER_ROW) % 2 == 1, second_half, found[8 * r : 8 * r + 8])

    copies[2].wait()
    st_ref[...] = jnp.transpose(s_ref[...].astype(F32))[:UNITS]
    low_table = jnp.concatenate([h256, h256], axis=1)
    high_table = jnp.concatenate([h256[:, : UNITS - 256], h256[:, : UNITS - 256]], axis=1)
    for e in range(EXAMPLES):
        copies[3 + 2 * e].wait()
        copies[4 + 2 * e].wait()
        signed = dot(c_ref[e], x_ref[e]) * st_ref[...]
        t = [signed[:, 128 * j : 128 * j + 128] for j in range(4)]
        a, b, c, d = t[0] + t[1], t[0] - t[1], t[2] + t[3], t[2] - t[3]
        part = slice(128 * e, 128 * e + 128)
        for j, value in enumerate((a + c, b + d, a - c, b - d)):
            high, low = split(value)
            split_ref[j, :256, part] = high[:256]
            split_ref[j, 256:512, part] = low[:256]
            split_ref[j, 512 : 256 + UNITS, part] = high[256:]
            split_ref[j, 256 + UNITS :, part] = low[256:]
    lanes2 = jnp.concatenate([lanes, lanes], axis=0)
    for j in range(4):
        first = dot(low_table, split_ref[j, :512])
        second = dot(high_table, split_ref[j, 512:])
        for upper, value in enumerate((first + second, first - second)):
            high, low = split(value)
            both = dot(jnp.concatenate([high, low], axis=1), lanes2)
            table[pl.ds(2 * j * COLS + 256 * upper, 256)] = both[:, :128]
            table[pl.ds((2 * j + 1) * COLS + 256 * upper, 256)] = both[:, 128:]
    q_copy.wait()

    place = lane & (NARROW - 1)

    def pick(target):
        block = ((target & 3) << 3) | (target >> 2)
        found = jnp.zeros((8, 128), F32)
        for half in range(2):
            r = block + half * FIRST
            for m in range(PER_ROW):
                rows = None
                for i in range(SECOND):
                    q = q_smem.at[:, pl.ds(i * PER_ROW + m, 1)][r, 0]
                    one = jnp.broadcast_to(table[pl.ds(q, 1), :], (8, 128))
                    rows = one if rows is None else jnp.where(sublane == i, one, rows)
                found = jnp.where(place == half * PER_ROW + m, permute(rows, index_ref[r, m]), found)
        return found * sign_ref[block]

    pl.semaphore_wait(barrier, FIRST + SECOND - 2)

    def send(step, target):
        pltpu.make_async_remote_copy(
            src_ref=send1.at[step], dst_ref=recv1.at[step], send_sem=send1_sem, recv_sem=recv1_sem,
            device_id=(grp, target), device_id_type=MESH,
        ).start()

    def produce(pair, targets):
        first, second = 2 * pair, 2 * pair + 1
        found = pick(targets[0]), pick(targets[1])
        send1[first], send1[second] = found
        send(first, targets[0])

        @pl.when(second < FIRST - 1)
        def _():
            send(second, targets[1])

        return peer1(first + 2), peer1(second + 2)

    lax.fori_loop(0, FIRST // 2, produce, (peer1(0), peer1(1)))
    pltpu.make_async_copy(recv1, recv1, recv1_sem).wait()
    total = send1[FIRST - 1]
    for step in range(FIRST - 1):
        total = total + recv1[step]
    for g in range(SECOND):
        send2[g] = total[g : g + 1]
    for step in range(SECOND - 1):
        target = peer2(step)
        pltpu.make_async_remote_copy(
            src_ref=send2.at[target], dst_ref=recv2.at[step], send_sem=send2_sem, recv_sem=recv2_sem,
            device_id=(target, shard), device_id_type=MESH,
        ).start()
    sent = send1.at[pl.ds(0, FIRST - 1)]
    pltpu.make_async_copy(sent, sent, send1_sem).wait()
    total = send2[grp]
    pltpu.make_async_copy(recv2, recv2, recv2_sem).wait()
    for step in range(SECOND - 1):
        total = total + recv2[step]
    for e in range(EXAMPLES):
        out_ref[e : e + 1, :] = total[:, NARROW * e : NARROW * e + KEPT // 256]
    pltpu.make_async_copy(recv2, recv2, send2_sem).wait()


def local(inputs, up_cotangent, signs, kept_row, kept_col):
    hbm = pl.BlockSpec(memory_space=pl.ANY)
    return pl.pallas_call(
        kernel,
        out_shape=jax.ShapeDtypeStruct((EXAMPLES, KEPT // 256), F32),
        in_specs=[hbm] * 5,
        out_specs=pl.BlockSpec(memory_space=pltpu.VMEM),
        scratch_shapes=[
            pltpu.VMEM((EXAMPLES, TOKENS, ROWS), BF16),
            pltpu.VMEM((EXAMPLES, UNITS, TOKENS), BF16),
            pltpu.VMEM((ROWS, COLS), jnp.int32),
            pltpu.VMEM((UNITS, ROWS), F32),
            pltpu.VMEM((64, 128), jnp.int32),
            pltpu.VMEM((64, 128), jnp.int32),
            pltpu.VMEM((64, 128), jnp.int32),
            pltpu.SMEM((64, 128), jnp.int32),
            pltpu.VMEM((64, PER_ROW, 8, 128), jnp.int32),
            pltpu.VMEM((FIRST, 8, 128), F32),
            pltpu.VMEM((4, 2 * UNITS, 256), BF16),
            pltpu.VMEM((8 * COLS, 128), F32),
            pltpu.VMEM((FIRST, 8, 128), F32),
            pltpu.VMEM((FIRST - 1, 8, 128), F32),
            pltpu.VMEM((SECOND, 1, 128), F32),
            pltpu.VMEM((SECOND - 1, 1, 128), F32),
            pltpu.SemaphoreType.DMA((8,)),
            pltpu.SemaphoreType.DMA,
            pltpu.SemaphoreType.DMA,
            pltpu.SemaphoreType.DMA,
            pltpu.SemaphoreType.DMA,
        ],
        compiler_params=pltpu.CompilerParams(
            vmem_limit_bytes=64 << 20, collective_id=0, has_side_effects=True
        ),
    )(inputs, jnp.swapaxes(up_cotangent, 1, 2), signs, kept_row.reshape(64, 128), kept_col.reshape(64, 128))


def solution(mesh):
    placed = (P(None, None, "grp"), P(None, None, "shard"), P("grp", "shard"), P(), P())
    return jax.shard_map(
        local, mesh=mesh, in_specs=placed, out_specs=P(None, ("grp", "shard")), check_vma=False
    )
```

```python
import math

import jax
import jax.numpy as jnp
from jax import lax
from jax.experimental import pallas as pl
from jax.experimental.pallas import tpu as pltpu
from jax.sharding import PartitionSpec as P

F32 = jnp.float32
BF16 = jnp.bfloat16
MESH = pl.DeviceIdType.MESH

EXAMPLES = 2
TOKENS = 1024
ROWS = 512
COLS = 512
UNITS = 448
KEPT = 8192
SCALE = 1.0 / math.sqrt(4096 * 16384)
FIRST = 32
SECOND = 8
NARROW = 64
PER_ROW = 16


def parity(bits):
    for shift in (8, 4, 2, 1):
        bits = bits ^ (bits >> shift)
    return bits & 1


def hadamard(shape):
    row = lax.broadcasted_iota(jnp.int32, shape, 0)
    col = lax.broadcasted_iota(jnp.int32, shape, 1)
    return jnp.where(parity(row & col) == 1, -1.0, 1.0).astype(BF16)


def lane_transform():
    row = lax.broadcasted_iota(jnp.int32, (256, 256), 0)
    col = lax.broadcasted_iota(jnp.int32, (256, 256), 1)
    target = ((col >> 7) << 6) | (col & 63)
    sign = jnp.where(parity((row & 127) & target) == 1, -1.0, 1.0)
    return jnp.where((row >> 7) == ((col >> 6) & 1), sign, 0.0).astype(BF16)


def split(values):
    high = values.astype(BF16)
    return high, (values - high.astype(F32)).astype(BF16)


def permute(values, index):
    numbers = lax.GatherDimensionNumbers(
        offset_dims=(), collapsed_slice_dims=(1,), start_index_map=(1,),
        operand_batching_dims=(0,), start_indices_batching_dims=(0,),
    )
    return lax.gather(values, index[..., None], numbers, (1, 1), mode=lax.GatherScatterMode.PROMISE_IN_BOUNDS)


def spread_table(columns, chosen):
    row = lax.broadcasted_iota(jnp.int32, (128, columns), 0)
    col = lax.broadcasted_iota(jnp.int32, (128, columns), 1)
    return jnp.where((row & (PER_ROW - 1)) == chosen(col), 1.0, 0.0).astype(BF16)


def dot(a, b):
    return jnp.dot(a, b, preferred_element_type=F32)


def kernel(
    x_hbm, c_hbm, s_hbm, row_hbm, col_hbm, out_ref,
    x_ref, c_ref, s_ref, st_ref, row_ref, col_ref, q_vmem, q_smem, index_ref, sign_ref, split_ref, table,
    send1, recv1, send2, recv2,
    sems, send1_sem, recv1_sem, send2_sem, recv2_sem,
):
    grp = lax.axis_index("grp")
    shard = lax.axis_index("shard")

    def peer1(step):
        return ((shard + 16 + (step << 3)) & 24) | (step >> 2)

    copies = [
        pltpu.make_async_copy(row_hbm, row_ref, sems.at[0]),
        pltpu.make_async_copy(col_hbm, col_ref, sems.at[1]),
        pltpu.make_async_copy(s_hbm, s_ref, sems.at[2]),
        pltpu.make_async_copy(x_hbm.at[0], x_ref.at[0], sems.at[3]),
        pltpu.make_async_copy(c_hbm.at[0], c_ref.at[0], sems.at[4]),
        pltpu.make_async_copy(x_hbm.at[1], x_ref.at[1], sems.at[5]),
        pltpu.make_async_copy(c_hbm.at[1], c_ref.at[1], sems.at[6]),
    ]
    for copy in copies:
        copy.start()

    barrier = pltpu.get_barrier_semaphore()

    def greet(step, carry):
        pl.semaphore_signal(barrier, inc=1, device_id=(grp, shard ^ step), device_id_type=MESH)
        return carry

    lax.fori_loop(1, FIRST, greet, 0)
    for step in range(1, SECOND):
        pl.semaphore_signal(barrier, inc=1, device_id=(grp ^ step, shard), device_id_type=MESH)

    h256 = hadamard((256, 256))
    lanes = lane_transform()

    copies[0].wait()
    copies[1].wait()
    row, col = row_ref[...], col_ref[...]
    device_bits = ((row >> 9) & grp) | (((col >> 9) & shard) << 3)
    entry = ((row & 511) >> 6) * COLS + (col & 511)
    packed = entry | ((row & (NARROW - 1)) << 12) | (parity(device_bits) << 18)
    lane = lax.broadcasted_iota(jnp.int32, (8, 128), 1)
    sublane = lax.broadcasted_iota(jnp.int32, (8, 128), 0)
    ordered = []
    for chunk in range(8):
        at = (chunk % 4) * 2 + chunk // 4
        value = None
        for i in range(SECOND):
            moved = packed[8 * i : 8 * i + 8]
            if i != at:
                moved = pltpu.roll(moved, ((i - at) % 8) * PER_ROW, 1)
            value = moved if value is None else jnp.where(lane // PER_ROW == i, moved, value)
        ordered.append(value)
    packed = jnp.concatenate(ordered, axis=0)
    q_vmem[...] = packed & 4095
    q_copy = pltpu.make_async_copy(q_vmem, q_smem, sems.at[7])
    q_copy.start()
    sign = jnp.where((packed >> 18) == 1, -1.0, 1.0)
    inner = ((packed >> 12) & (NARROW - 1)).astype(F32)
    mine = (lane // PER_ROW) == sublane

    def diagonal(values):
        blocks = [jnp.where(mine, jnp.broadcast_to(values[r : r + 1], (8, 128)), 0.0) for r in range(64)]
        return jnp.concatenate(blocks, axis=0).astype(BF16)

    spots = diagonal(inner)
    for pair in range(PER_ROW // 2):
        found = dot(spots, spread_table(256, lambda y: 2 * pair + (y >> 7))).astype(jnp.int32)
        for u in range(2):
            part = found[:, 128 * u : 128 * u + 128].reshape(64, 8, 128)
            index_ref[:, 2 * pair + u] = part + (lane & NARROW)[None]
    found = dot(diagonal(sign), spread_table(128, lambda y: y & (PER_ROW - 1))) * SCALE
    for r in range(FIRST):
        second_half = found[8 * (FIRST + r) : 8 * (FIRST + r) + 8]
        sign_ref[r] = jnp.where((lane // PER_ROW) % 2 == 1, second_half, found[8 * r : 8 * r + 8])

    copies[2].wait()
    st_ref[...] = jnp.transpose(s_ref[...].astype(F32))[:UNITS]
    low_table = jnp.concatenate([h256, h256], axis=1)
    high_table = jnp.concatenate([h256[:, : UNITS - 256], h256[:, : UNITS - 256]], axis=1)
    for e in range(EXAMPLES):
        copies[3 + 2 * e].wait()
        copies[4 + 2 * e].wait()
        signed = dot(c_ref[e], x_ref[e]) * st_ref[...]
        t = [signed[:, 128 * j : 128 * j + 128] for j in range(4)]
        a, b, c, d = t[0] + t[1], t[0] - t[1], t[2] + t[3], t[2] - t[3]
        part = slice(128 * e, 128 * e + 128)
        for j, value in enumerate((a + c, b + d, a - c, b - d)):
            high, low = split(value)
            split_ref[j, :256, part] = high[:256]
            split_ref[j, 256:512, part] = low[:256]
            split_ref[j, 512 : 256 + UNITS, part] = high[256:]
            split_ref[j, 256 + UNITS :, part] = low[256:]
    lanes2 = jnp.concatenate([lanes, lanes], axis=0)
    for j in range(4):
        first = dot(low_table, split_ref[j, :512])
        second = dot(high_table, split_ref[j, 512:])
        for upper, value in enumerate((first + second, first - second)):
            high, low = split(value)
            both = dot(jnp.concatenate([high, low], axis=1), lanes2)
            table[pl.ds(2 * j * COLS + 256 * upper, 256)] = both[:, :128]
            table[pl.ds((2 * j + 1) * COLS + 256 * upper, 256)] = both[:, 128:]
    q_copy.wait()

    place = lane & (NARROW - 1)

    def pick(target):
        block = ((target & 3) << 3) | (target >> 2)
        found = jnp.zeros((8, 128), F32)
        for half in range(2):
            r = block + half * FIRST
            for m in range(PER_ROW):
                rows = None
                for i in range(SECOND):
                    q = q_smem.at[:, pl.ds(i * PER_ROW + m, 1)][r, 0]
                    one = jnp.broadcast_to(table[pl.ds(q, 1), :], (8, 128))
                    rows = one if rows is None else jnp.where(sublane == i, one, rows)
                found = jnp.where(place == half * PER_ROW + m, permute(rows, index_ref[r, m]), found)
        return found * sign_ref[block]

    pl.semaphore_wait(barrier, FIRST + SECOND - 2)

    def deliver(step, target):
        @pl.when(target != shard)
        def _():
            pltpu.make_async_remote_copy(
                src_ref=send1.at[step], dst_ref=recv1.at[shard], send_sem=send1_sem, recv_sem=recv1_sem,
                device_id=(grp, target), device_id_type=MESH,
            ).start()

        @pl.when(target == shard)
        def _():
            recv1[shard] = send1[step]

    def produce(pair, carry):
        first, second = 2 * pair, 2 * pair + 1
        found = pick(peer1(first)), pick(peer1(second))
        send1[first], send1[second] = found
        deliver(first, peer1(first))
        deliver(second, peer1(second))
        return carry

    lax.fori_loop(0, FIRST // 2, produce, 0)
    sent = send1.at[pl.ds(0, FIRST - 1)]
    pltpu.make_async_copy(sent, sent, recv1_sem).wait()
    total = recv1[0]
    for source in range(1, FIRST):
        total = total + recv1[source]
    for target in range(SECOND):
        send2[target] = total[target : target + 1]
    for target in range(SECOND):

        @pl.when(target != grp)
        def _():
            pltpu.make_async_remote_copy(
                src_ref=send2.at[target], dst_ref=recv2.at[grp], send_sem=send2_sem, recv_sem=recv2_sem,
                device_id=(target, shard), device_id_type=MESH,
            ).start()

    recv2[grp] = send2[grp]
    pltpu.make_async_copy(sent, sent, send1_sem).wait()
    others = send2.at[pl.ds(0, SECOND - 1)]
    pltpu.make_async_copy(others, others, recv2_sem).wait()
    total = recv2[0]
    for source in range(1, SECOND):
        total = total + recv2[source]
    for e in range(EXAMPLES):
        out_ref[e : e + 1, :] = total[:, NARROW * e : NARROW * e + KEPT // 256]
    pltpu.make_async_copy(others, others, send2_sem).wait()


def local(inputs, up_cotangent, signs, kept_row, kept_col):
    hbm = pl.BlockSpec(memory_space=pl.ANY)
    return pl.pallas_call(
        kernel,
        out_shape=jax.ShapeDtypeStruct((EXAMPLES, KEPT // 256), F32),
        in_specs=[hbm] * 5,
        out_specs=pl.BlockSpec(memory_space=pltpu.VMEM),
        scratch_shapes=[
            pltpu.VMEM((EXAMPLES, TOKENS, ROWS), BF16),
            pltpu.VMEM((EXAMPLES, UNITS, TOKENS), BF16),
            pltpu.VMEM((ROWS, COLS), jnp.int32),
            pltpu.VMEM((UNITS, ROWS), F32),
            pltpu.VMEM((64, 128), jnp.int32),
            pltpu.VMEM((64, 128), jnp.int32),
            pltpu.VMEM((64, 128), jnp.int32),
            pltpu.SMEM((64, 128), jnp.int32),
            pltpu.VMEM((64, PER_ROW, 8, 128), jnp.int32),
            pltpu.VMEM((FIRST, 8, 128), F32),
            pltpu.VMEM((4, 2 * UNITS, 256), BF16),
            pltpu.VMEM((8 * COLS, 128), F32),
            pltpu.VMEM((FIRST, 8, 128), F32),
            pltpu.VMEM((FIRST, 8, 128), F32),
            pltpu.VMEM((SECOND, 1, 128), F32),
            pltpu.VMEM((SECOND, 1, 128), F32),
            pltpu.SemaphoreType.DMA((8,)),
            pltpu.SemaphoreType.DMA,
            pltpu.SemaphoreType.DMA,
            pltpu.SemaphoreType.DMA,
            pltpu.SemaphoreType.DMA,
        ],
        compiler_params=pltpu.CompilerParams(
            vmem_limit_bytes=32 << 20, collective_id=0, has_side_effects=True
        ),
    )(*[
        pltpu.with_memory_space_constraint(array, pltpu.HBM)
        for array in (inputs, jnp.swapaxes(up_cotangent, 1, 2), signs, kept_row.reshape(64, 128), kept_col.reshape(64, 128))
    ])


def solution(mesh):
    placed = (P(None, None, "grp"), P(None, None, "shard"), P("grp", "shard"), P(), P())
    return jax.shard_map(
        local, mesh=mesh, in_specs=placed, out_specs=P(None, ("grp", "shard")), check_vma=False
    )
```

```python
import math

import jax
import jax.numpy as jnp
from jax import lax
from jax.experimental import pallas as pl
from jax.experimental.pallas import tpu as pltpu
from jax.sharding import PartitionSpec as P

F32 = jnp.float32
BF16 = jnp.bfloat16
MESH = pl.DeviceIdType.MESH

EXAMPLES = 2
TOKENS = 1024
ROWS = 512
COLS = 512
UNITS = 448
KEPT = 8192
SCALE = 1.0 / math.sqrt(4096 * 16384)
FIRST = 32
SECOND = 8
NARROW = 64
PER_ROW = 16


def parity(bits):
    for shift in (8, 4, 2, 1):
        bits = bits ^ (bits >> shift)
    return bits & 1


def hadamard(shape):
    row = lax.broadcasted_iota(jnp.int32, shape, 0)
    col = lax.broadcasted_iota(jnp.int32, shape, 1)
    return jnp.where(parity(row & col) == 1, -1.0, 1.0).astype(BF16)


def lane_transform():
    row = lax.broadcasted_iota(jnp.int32, (256, 256), 0)
    col = lax.broadcasted_iota(jnp.int32, (256, 256), 1)
    target = ((col >> 7) << 6) | (col & 63)
    sign = jnp.where(parity((row & 127) & target) == 1, -1.0, 1.0)
    return jnp.where((row >> 7) == ((col >> 6) & 1), sign, 0.0).astype(BF16)


def split(values):
    high = values.astype(BF16)
    return high, (values - high.astype(F32)).astype(BF16)


def permute(values, index):
    numbers = lax.GatherDimensionNumbers(
        offset_dims=(), collapsed_slice_dims=(1,), start_index_map=(1,),
        operand_batching_dims=(0,), start_indices_batching_dims=(0,),
    )
    return lax.gather(values, index[..., None], numbers, (1, 1), mode=lax.GatherScatterMode.PROMISE_IN_BOUNDS)


def spread_table(columns, chosen):
    row = lax.broadcasted_iota(jnp.int32, (128, columns), 0)
    col = lax.broadcasted_iota(jnp.int32, (128, columns), 1)
    return jnp.where((row & (PER_ROW - 1)) == chosen(col), 1.0, 0.0).astype(BF16)


def dot(a, b):
    return jnp.dot(a, b, preferred_element_type=F32)


def kernel(
    x_hbm, c_hbm, s_hbm, row_hbm, col_hbm, out_ref,
    x_ref, c_ref, s_ref, st_ref, row_ref, col_ref, q_vmem, q_smem, index_ref, sign_ref, split_ref, half_ref, table,
    send1, recv1, send2, recv2,
    sems, send1_sem, recv1_sem, send2_sem, recv2_sem,
):
    grp = lax.axis_index("grp")
    shard = lax.axis_index("shard")

    def peer1(step):
        return ((shard + 8 + (step << 3)) & 24) | (step >> 2)

    copies = [
        pltpu.make_async_copy(row_hbm, row_ref, sems.at[0]),
        pltpu.make_async_copy(col_hbm, col_ref, sems.at[1]),
        pltpu.make_async_copy(s_hbm, s_ref, sems.at[2]),
        pltpu.make_async_copy(x_hbm.at[0], x_ref.at[0], sems.at[3]),
        pltpu.make_async_copy(c_hbm.at[0], c_ref.at[0], sems.at[4]),
        pltpu.make_async_copy(x_hbm.at[1], x_ref.at[1], sems.at[5]),
        pltpu.make_async_copy(c_hbm.at[1], c_ref.at[1], sems.at[6]),
    ]
    for copy in copies:
        copy.start()

    barrier = pltpu.get_barrier_semaphore()

    def greet(step, carry):
        pl.semaphore_signal(barrier, inc=1, device_id=(grp, shard ^ step), device_id_type=MESH)
        return carry

    lax.fori_loop(1, FIRST, greet, 0)
    for step in range(1, SECOND):
        pl.semaphore_signal(barrier, inc=1, device_id=(grp ^ step, shard), device_id_type=MESH)

    h128 = hadamard((128, 128))
    lanes = lane_transform()

    copies[0].wait()
    copies[1].wait()
    row, col = row_ref[...], col_ref[...]
    device_bits = ((row >> 9) & grp) | (((col >> 9) & shard) << 3)
    entry = ((row & 511) >> 6) * COLS + (col & 511)
    packed = entry | ((row & (NARROW - 1)) << 12) | (parity(device_bits) << 18)
    lane = lax.broadcasted_iota(jnp.int32, (8, 128), 1)
    sublane = lax.broadcasted_iota(jnp.int32, (8, 128), 0)
    ordered = []
    for chunk in range(8):
        at = (chunk % 4) * 2 + chunk // 4
        value = None
        for i in range(SECOND):
            moved = packed[8 * i : 8 * i + 8]
            if i != at:
                moved = pltpu.roll(moved, ((i - at) % 8) * PER_ROW, 1)
            value = moved if value is None else jnp.where(lane // PER_ROW == i, moved, value)
        ordered.append(value)
    packed = jnp.concatenate(ordered, axis=0)
    q_vmem[...] = packed & 4095
    q_copy = pltpu.make_async_copy(q_vmem, q_smem, sems.at[7])
    q_copy.start()
    sign = jnp.where((packed >> 18) == 1, -1.0, 1.0)
    inner = ((packed >> 12) & (NARROW - 1)).astype(F32)
    mine = (lane // PER_ROW) == sublane

    def diagonal(values):
        blocks = [jnp.where(mine, jnp.broadcast_to(values[r : r + 1], (8, 128)), 0.0) for r in range(64)]
        return jnp.concatenate(blocks, axis=0).astype(BF16)

    spots = diagonal(inner)
    for pair in range(PER_ROW // 2):
        found = dot(spots, spread_table(256, lambda y: 2 * pair + (y >> 7))).astype(jnp.int32)
        for u in range(2):
            part = found[:, 128 * u : 128 * u + 128].reshape(64, 8, 128)
            index_ref[:, 2 * pair + u] = part + (lane & NARROW)[None]
    found = dot(diagonal(sign), spread_table(128, lambda y: y & (PER_ROW - 1))) * SCALE
    for r in range(FIRST):
        second_half = found[8 * (FIRST + r) : 8 * (FIRST + r) + 8]
        sign_ref[r] = jnp.where((lane // PER_ROW) % 2 == 1, second_half, found[8 * r : 8 * r + 8])

    copies[2].wait()
    st_ref[...] = jnp.transpose(s_ref[...].astype(F32))[:UNITS]
    for e in range(EXAMPLES):
        copies[3 + 2 * e].wait()
        copies[4 + 2 * e].wait()
        signed = dot(c_ref[e], x_ref[e]) * st_ref[...]
        t = [signed[:, 128 * j : 128 * j + 128] for j in range(4)]
        a, b, c, d = t[0] + t[1], t[0] - t[1], t[2] + t[3], t[2] - t[3]
        part = slice(128 * e, 128 * e + 128)
        for j, value in enumerate((a + c, b + d, a - c, b - d)):
            for block in range(4):
                rows = slice(128 * block, min(128 * block + 128, UNITS))
                high, low = split(value[rows])
                size = high.shape[0]
                split_ref[j, 256 * block : 256 * block + size, part] = high
                split_ref[j, 256 * block + size : 256 * block + 2 * size, part] = low
    full = jnp.concatenate([h128, h128], axis=1)
    short = jnp.concatenate([h128[:, : UNITS - 384], h128[:, : UNITS - 384]], axis=1)
    for j in range(4):
        t = [dot(full, split_ref[j, 256 * block : 256 * block + 256]) for block in range(3)]
        t.append(dot(short, split_ref[j, 768:]))
        a, b, c, d = t[0] + t[1], t[0] - t[1], t[2] + t[3], t[2] - t[3]
        for block, value in enumerate((a + c, b + d, a - c, b - d)):
            rows = slice(128 * block, 128 * block + 128)
            high, low = split(value)
            half_ref[j, rows, :256] = high
            half_ref[j, rows, 256:] = low
    lanes2 = jnp.concatenate([lanes, lanes], axis=0)
    for j in range(4):
        both = dot(half_ref[j], lanes2)
        table[pl.ds(2 * j * COLS, COLS)] = both[:, :128]
        table[pl.ds((2 * j + 1) * COLS, COLS)] = both[:, 128:]
    q_copy.wait()

    place = lane & (NARROW - 1)

    def pick(target):
        block = ((target & 3) << 3) | (target >> 2)
        found = jnp.zeros((8, 128), F32)
        for half in range(2):
            r = block + half * FIRST
            for m in range(PER_ROW):
                rows = None
                for i in range(SECOND):
                    q = q_smem.at[:, pl.ds(i * PER_ROW + m, 1)][r, 0]
                    one = jnp.broadcast_to(table[pl.ds(q, 1), :], (8, 128))
                    rows = one if rows is None else jnp.where(sublane == i, one, rows)
                found = jnp.where(place == half * PER_ROW + m, permute(rows, index_ref[r, m]), found)
        return found * sign_ref[block]

    pl.semaphore_wait(barrier, FIRST + SECOND - 2)

    def deliver(step, target):
        @pl.when(target != shard)
        def _():
            pltpu.make_async_remote_copy(
                src_ref=send1.at[step], dst_ref=recv1.at[shard], send_sem=send1_sem, recv_sem=recv1_sem,
                device_id=(grp, target), device_id_type=MESH,
            ).start()

        @pl.when(target == shard)
        def _():
            recv1[shard] = send1[step]

    def produce(pair, carry):
        first, second = 2 * pair, 2 * pair + 1
        found = pick(peer1(first)), pick(peer1(second))
        send1[first], send1[second] = found
        deliver(first, peer1(first))
        deliver(second, peer1(second))
        return carry

    lax.fori_loop(0, FIRST // 2, produce, 0)
    sent = send1.at[pl.ds(0, FIRST - 1)]
    pltpu.make_async_copy(sent, sent, recv1_sem).wait()
    total = recv1[0]
    for source in range(1, FIRST):
        total = total + recv1[source]
    for row in range(SECOND):
        send2[row] = total[row : row + 1]
    for target in (1, 0, 2, 3, 6, 7, 4, 5):

        @pl.when(target != grp)
        def _():
            pltpu.make_async_remote_copy(
                src_ref=send2.at[target], dst_ref=recv2.at[grp], send_sem=send2_sem, recv_sem=recv2_sem,
                device_id=(target, shard), device_id_type=MESH,
            ).start()

    recv2[grp] = send2[grp]
    pltpu.make_async_copy(sent, sent, send1_sem).wait()
    others = recv2.at[pl.ds(0, SECOND - 1)]
    pltpu.make_async_copy(others, others, recv2_sem).wait()
    total = recv2[0]
    for source in range(1, SECOND):
        total = total + recv2[source]
    for e in range(EXAMPLES):
        out_ref[e : e + 1, :] = total[:, NARROW * e : NARROW * e + KEPT // 256]
    pltpu.make_async_copy(others, others, send2_sem).wait()


def local(inputs, up_cotangent, signs, kept_row, kept_col):
    hbm = pl.BlockSpec(memory_space=pl.ANY)
    return pl.pallas_call(
        kernel,
        out_shape=jax.ShapeDtypeStruct((EXAMPLES, KEPT // 256), F32),
        in_specs=[hbm] * 5,
        out_specs=pl.BlockSpec(memory_space=pltpu.VMEM),
        scratch_shapes=[
            pltpu.VMEM((EXAMPLES, TOKENS, ROWS), BF16),
            pltpu.VMEM((EXAMPLES, UNITS, TOKENS), BF16),
            pltpu.VMEM((ROWS, COLS), jnp.int32),
            pltpu.VMEM((UNITS, ROWS), F32),
            pltpu.VMEM((64, 128), jnp.int32),
            pltpu.VMEM((64, 128), jnp.int32),
            pltpu.VMEM((64, 128), jnp.int32),
            pltpu.SMEM((64, 128), jnp.int32),
            pltpu.VMEM((64, PER_ROW, 8, 128), jnp.int32),
            pltpu.VMEM((FIRST, 8, 128), F32),
            pltpu.VMEM((4, 2 * UNITS, 256), BF16),
            pltpu.VMEM((4, COLS, 512), BF16),
            pltpu.VMEM((8 * COLS, 128), F32),
            pltpu.VMEM((FIRST, 8, 128), F32),
            pltpu.VMEM((FIRST, 8, 128), F32),
            pltpu.VMEM((SECOND, 1, 128), F32),
            pltpu.VMEM((SECOND, 1, 128), F32),
            pltpu.SemaphoreType.DMA((8,)),
            pltpu.SemaphoreType.DMA,
            pltpu.SemaphoreType.DMA,
            pltpu.SemaphoreType.DMA,
            pltpu.SemaphoreType.DMA,
        ],
        compiler_params=pltpu.CompilerParams(
            vmem_limit_bytes=32 << 20, collective_id=0, has_side_effects=True
        ),
    )(*[
        pltpu.with_memory_space_constraint(array, pltpu.HBM)
        for array in (inputs, jnp.swapaxes(up_cotangent, 1, 2), signs, kept_row.reshape(64, 128), kept_col.reshape(64, 128))
    ])


def solution(mesh):
    placed = (P(None, None, "grp"), P(None, None, "shard"), P("grp", "shard"), P(), P())
    return jax.shard_map(
        local, mesh=mesh, in_specs=placed, out_specs=P(None, ("grp", "shard")), check_vma=False
    )
```

```python
import math

import jax
import jax.numpy as jnp
from jax import lax
from jax.experimental import pallas as pl
from jax.experimental.pallas import tpu as pltpu
from jax.sharding import PartitionSpec as P

F32 = jnp.float32
BF16 = jnp.bfloat16
MESH = pl.DeviceIdType.MESH

EXAMPLES = 2
TOKENS = 1024
ROWS = 512
COLS = 512
UNITS = 448
KEPT = 8192
SCALE = 1.0 / math.sqrt(4096 * 16384)
FIRST = 32
SECOND = 8
NARROW = 64
PER_ROW = 16


def parity(bits):
    for shift in (8, 4, 2, 1):
        bits = bits ^ (bits >> shift)
    return bits & 1


def hadamard(shape):
    row = lax.broadcasted_iota(jnp.int32, shape, 0)
    col = lax.broadcasted_iota(jnp.int32, shape, 1)
    return jnp.where(parity(row & col) == 1, -1.0, 1.0).astype(BF16)


def lane_transform():
    row = lax.broadcasted_iota(jnp.int32, (256, 256), 0)
    col = lax.broadcasted_iota(jnp.int32, (256, 256), 1)
    target = ((col >> 7) << 6) | (col & 63)
    sign = jnp.where(parity((row & 127) & target) == 1, -1.0, 1.0)
    return jnp.where((row >> 7) == ((col >> 6) & 1), sign, 0.0).astype(BF16)


def split(values):
    high = values.astype(BF16)
    return high, (values - high.astype(F32)).astype(BF16)


def permute(values, index):
    numbers = lax.GatherDimensionNumbers(
        offset_dims=(), collapsed_slice_dims=(1,), start_index_map=(1,),
        operand_batching_dims=(0,), start_indices_batching_dims=(0,),
    )
    return lax.gather(values, index[..., None], numbers, (1, 1), mode=lax.GatherScatterMode.PROMISE_IN_BOUNDS)


def spread_table(columns, chosen):
    row = lax.broadcasted_iota(jnp.int32, (128, columns), 0)
    col = lax.broadcasted_iota(jnp.int32, (128, columns), 1)
    return jnp.where((row & (PER_ROW - 1)) == chosen(col), 1.0, 0.0).astype(BF16)


def dot(a, b):
    return jnp.dot(a, b, preferred_element_type=F32)


def kernel(
    x_hbm, c_hbm, s_hbm, row_hbm, col_hbm, out_ref,
    x_ref, c_ref, s_ref, st_ref, row_ref, col_ref, q_vmem, q_smem, index_ref, sign_ref, split_ref, half_ref, table,
    send1, recv1, send2, recv2,
    sems, send1_sem, recv1_sem, send2_sem, recv2_sem,
):
    grp = lax.axis_index("grp")
    shard = lax.axis_index("shard")

    def peer1(step):
        return ((shard + 8 + (step << 3)) & 24) | (step >> 2)

    copies = [
        pltpu.make_async_copy(row_hbm, row_ref, sems.at[0]),
        pltpu.make_async_copy(col_hbm, col_ref, sems.at[1]),
        pltpu.make_async_copy(s_hbm, s_ref, sems.at[2]),
        pltpu.make_async_copy(x_hbm.at[0], x_ref.at[0], sems.at[3]),
        pltpu.make_async_copy(c_hbm.at[0], c_ref.at[0], sems.at[4]),
        pltpu.make_async_copy(x_hbm.at[1], x_ref.at[1], sems.at[5]),
        pltpu.make_async_copy(c_hbm.at[1], c_ref.at[1], sems.at[6]),
    ]
    for copy in copies:
        copy.start()

    barrier = pltpu.get_barrier_semaphore()

    def greet(step, carry):
        target = ((shard + (step << 3)) & 24) | (step >> 2)

        @pl.when(target != shard)
        def _():
            pl.semaphore_signal(barrier, inc=1, device_id=(grp, target), device_id_type=MESH)

        return carry

    lax.fori_loop(0, FIRST, greet, 0)
    for step in range(1, SECOND):
        pl.semaphore_signal(barrier, inc=1, device_id=(grp ^ step, shard), device_id_type=MESH)

    h128 = hadamard((128, 128))
    lanes = lane_transform()

    copies[0].wait()
    copies[1].wait()
    row, col = row_ref[...], col_ref[...]
    device_bits = ((row >> 9) & grp) | (((col >> 9) & shard) << 3)
    entry = ((row & 511) >> 6) * COLS + (col & 511)
    packed = entry | ((row & (NARROW - 1)) << 12) | (parity(device_bits) << 18)
    lane = lax.broadcasted_iota(jnp.int32, (8, 128), 1)
    sublane = lax.broadcasted_iota(jnp.int32, (8, 128), 0)
    ordered = []
    for chunk in range(8):
        at = (chunk % 4) * 2 + chunk // 4
        value = None
        for i in range(SECOND):
            moved = packed[8 * i : 8 * i + 8]
            if i != at:
                moved = pltpu.roll(moved, ((i - at) % 8) * PER_ROW, 1)
            value = moved if value is None else jnp.where(lane // PER_ROW == i, moved, value)
        ordered.append(value)
    packed = jnp.concatenate(ordered, axis=0)
    q_vmem[...] = packed & 4095
    q_copy = pltpu.make_async_copy(q_vmem, q_smem, sems.at[7])
    q_copy.start()
    marks = (((packed >> 12) & (NARROW - 1)) | ((packed >> 18) << 7)).astype(F32)
    mine = (lane // PER_ROW) == sublane

    def diagonal(values):
        blocks = [jnp.where(mine, jnp.broadcast_to(values[r : r + 1], (8, 128)), 0.0) for r in range(64)]
        return jnp.concatenate(blocks, axis=0).astype(BF16)

    found = dot(diagonal(marks), spread_table(128, lambda y: y & (PER_ROW - 1))).astype(jnp.int32)
    for r in range(FIRST):
        second_half = found[8 * (FIRST + r) : 8 * (FIRST + r) + 8]
        mark = jnp.where((lane // PER_ROW) % 2 == 1, second_half, found[8 * r : 8 * r + 8])
        index_ref[r] = (mark & (NARROW - 1)) | (lane & NARROW)
        sign_ref[r] = jnp.where(mark >= 128, -SCALE, SCALE)

    copies[2].wait()
    st_ref[...] = jnp.transpose(s_ref[...].astype(F32))[:UNITS]
    for e in range(EXAMPLES):
        copies[3 + 2 * e].wait()
        copies[4 + 2 * e].wait()
        signed = dot(c_ref[e], x_ref[e]) * st_ref[...]
        t = [signed[:, 128 * j : 128 * j + 128] for j in range(4)]
        a, b, c, d = t[0] + t[1], t[0] - t[1], t[2] + t[3], t[2] - t[3]
        part = slice(128 * e, 128 * e + 128)
        for j, value in enumerate((a + c, b + d, a - c, b - d)):
            for block in range(4):
                rows = slice(128 * block, min(128 * block + 128, UNITS))
                high, low = split(value[rows])
                size = high.shape[0]
                split_ref[j, 256 * block : 256 * block + size, part] = high
                split_ref[j, 256 * block + size : 256 * block + 2 * size, part] = low
    full = jnp.concatenate([h128, h128], axis=1)
    short = jnp.concatenate([h128[:, : UNITS - 384], h128[:, : UNITS - 384]], axis=1)
    for j in range(4):
        t = [dot(full, split_ref[j, 256 * block : 256 * block + 256]) for block in range(3)]
        t.append(dot(short, split_ref[j, 768:]))
        a, b, c, d = t[0] + t[1], t[0] - t[1], t[2] + t[3], t[2] - t[3]
        for block, value in enumerate((a + c, b + d, a - c, b - d)):
            rows = slice(128 * block, 128 * block + 128)
            high, low = split(value)
            half_ref[j, rows, :256] = high
            half_ref[j, rows, 256:] = low
    lanes2 = jnp.concatenate([lanes, lanes], axis=0)
    for j in range(4):
        both = dot(half_ref[j], lanes2)
        table[pl.ds(2 * j * COLS, COLS)] = both[:, :128]
        table[pl.ds((2 * j + 1) * COLS, COLS)] = both[:, 128:]
    q_copy.wait()

    place = lane & (NARROW - 1)

    def pick(target):
        block = ((target & 3) << 3) | (target >> 2)
        index = index_ref[block]
        found = jnp.zeros((8, 128), F32)
        for half in range(2):
            r = block + half * FIRST
            for m in range(PER_ROW):
                rows = None
                for i in range(SECOND):
                    q = q_smem.at[:, pl.ds(i * PER_ROW + m, 1)][r, 0]
                    one = jnp.broadcast_to(table[pl.ds(q, 1), :], (8, 128))
                    rows = one if rows is None else jnp.where(sublane == i, one, rows)
                found = jnp.where(place == half * PER_ROW + m, permute(rows, index), found)
        return found * sign_ref[block]

    def deliver(step, carry):
        target = peer1(step)

        @pl.when(target != shard)
        def _():
            pltpu.make_async_remote_copy(
                src_ref=send1.at[step], dst_ref=recv1.at[shard], send_sem=send1_sem, recv_sem=recv1_sem,
                device_id=(grp, target), device_id_type=MESH,
            ).start()

        @pl.when(target == shard)
        def _():
            recv1[shard] = send1[step]

        return carry

    depth = shard & 7
    meet = jnp.where(depth >= 4, 0, 9 - (5 * depth) // 2)

    def produce(pair, carry):
        first, second = 2 * pair, 2 * pair + 1
        found = pick(peer1(first)), pick(peer1(second))
        send1[first], send1[second] = found

        @pl.when(pair == meet)
        def _():
            pl.semaphore_wait(barrier, FIRST + SECOND - 2)

        @pl.when(pair >= meet)
        def _():
            lax.fori_loop(jnp.where(pair == meet, 0, first), second + 1, deliver, 0)

        return carry

    lax.fori_loop(0, FIRST // 2, produce, 0)
    sent = send1.at[pl.ds(0, FIRST - 1)]
    pltpu.make_async_copy(sent, sent, recv1_sem).wait()
    total = recv1[0]
    for source in range(1, FIRST):
        total = total + recv1[source]
    for row in range(SECOND):
        send2[row] = total[row : row + 1]
    for target in (1, 0, 2, 3, 6, 7, 4, 5):

        @pl.when(target != grp)
        def _():
            pltpu.make_async_remote_copy(
                src_ref=send2.at[target], dst_ref=recv2.at[grp], send_sem=send2_sem, recv_sem=recv2_sem,
                device_id=(target, shard), device_id_type=MESH,
            ).start()

    recv2[grp] = send2[grp]
    others = recv2.at[pl.ds(0, SECOND - 1)]
    pltpu.make_async_copy(others, others, recv2_sem).wait()
    total = recv2[0]
    for source in range(1, SECOND):
        total = total + recv2[source]
    for e in range(EXAMPLES):
        out_ref[e : e + 1, :] = total[:, NARROW * e : NARROW * e + KEPT // 256]
    pltpu.make_async_copy(sent, sent, send1_sem).wait()
    pltpu.make_async_copy(others, others, send2_sem).wait()


def local(inputs, up_cotangent, signs, kept_row, kept_col):
    hbm = pl.BlockSpec(memory_space=pl.ANY)
    return pl.pallas_call(
        kernel,
        out_shape=jax.ShapeDtypeStruct((EXAMPLES, KEPT // 256), F32),
        in_specs=[hbm] * 5,
        out_specs=pl.BlockSpec(memory_space=pltpu.VMEM),
        scratch_shapes=[
            pltpu.VMEM((EXAMPLES, TOKENS, ROWS), BF16),
            pltpu.VMEM((EXAMPLES, UNITS, TOKENS), BF16),
            pltpu.VMEM((ROWS, COLS), jnp.int32),
            pltpu.VMEM((UNITS, ROWS), F32),
            pltpu.VMEM((64, 128), jnp.int32),
            pltpu.VMEM((64, 128), jnp.int32),
            pltpu.VMEM((64, 128), jnp.int32),
            pltpu.SMEM((64, 128), jnp.int32),
            pltpu.VMEM((FIRST, 8, 128), jnp.int32),
            pltpu.VMEM((FIRST, 8, 128), F32),
            pltpu.VMEM((4, 2 * UNITS, 256), BF16),
            pltpu.VMEM((4, COLS, 512), BF16),
            pltpu.VMEM((8 * COLS, 128), F32),
            pltpu.VMEM((FIRST, 8, 128), F32),
            pltpu.VMEM((FIRST, 8, 128), F32),
            pltpu.VMEM((SECOND, 1, 128), F32),
            pltpu.VMEM((SECOND, 1, 128), F32),
            pltpu.SemaphoreType.DMA((8,)),
            pltpu.SemaphoreType.DMA,
            pltpu.SemaphoreType.DMA,
            pltpu.SemaphoreType.DMA,
            pltpu.SemaphoreType.DMA,
        ],
        compiler_params=pltpu.CompilerParams(
            vmem_limit_bytes=32 << 20, collective_id=0, has_side_effects=True
        ),
    )(*[
        pltpu.with_memory_space_constraint(array, pltpu.HBM)
        for array in (inputs, jnp.swapaxes(up_cotangent, 1, 2), signs, kept_row.reshape(64, 128), kept_col.reshape(64, 128))
    ])


def solution(mesh):
    placed = (P(None, None, "grp"), P(None, None, "shard"), P("grp", "shard"), P(), P())
    return jax.shard_map(
        local, mesh=mesh, in_specs=placed, out_specs=P(None, ("grp", "shard")), check_vma=False
    )
```

```python
import math

import jax
import jax.numpy as jnp
from jax import lax
from jax.experimental import pallas as pl
from jax.experimental.pallas import tpu as pltpu
from jax.sharding import PartitionSpec as P

F32 = jnp.float32
BF16 = jnp.bfloat16
MESH = pl.DeviceIdType.MESH

EXAMPLES = 2
TOKENS = 1024
ROWS = 512
COLS = 512
UNITS = 448
KEPT = 8192
SCALE = 1.0 / math.sqrt(4096 * 16384)
FIRST = 32
SECOND = 8
DIRECT = 2
NARROW = 64
PER_ROW = 16


def parity(bits):
    for shift in (8, 4, 2, 1):
        bits = bits ^ (bits >> shift)
    return bits & 1


def hadamard(shape):
    row = lax.broadcasted_iota(jnp.int32, shape, 0)
    col = lax.broadcasted_iota(jnp.int32, shape, 1)
    return jnp.where(parity(row & col) == 1, -1.0, 1.0).astype(BF16)


def lane_transform():
    row = lax.broadcasted_iota(jnp.int32, (256, 256), 0)
    col = lax.broadcasted_iota(jnp.int32, (256, 256), 1)
    target = ((col >> 7) << 6) | (col & 63)
    sign = jnp.where(parity((row & 127) & target) == 1, -1.0, 1.0)
    return jnp.where((row >> 7) == ((col >> 6) & 1), sign, 0.0).astype(BF16)


def split(values):
    high = values.astype(BF16)
    return high, (values - high.astype(F32)).astype(BF16)


def permute(values, index):
    numbers = lax.GatherDimensionNumbers(
        offset_dims=(), collapsed_slice_dims=(1,), start_index_map=(1,),
        operand_batching_dims=(0,), start_indices_batching_dims=(0,),
    )
    return lax.gather(values, index[..., None], numbers, (1, 1), mode=lax.GatherScatterMode.PROMISE_IN_BOUNDS)


def spread_table(columns, chosen):
    row = lax.broadcasted_iota(jnp.int32, (128, columns), 0)
    col = lax.broadcasted_iota(jnp.int32, (128, columns), 1)
    return jnp.where((row & (PER_ROW - 1)) == chosen(col), 1.0, 0.0).astype(BF16)


def dot(a, b):
    return jnp.dot(a, b, preferred_element_type=F32)


def kernel(
    x_hbm, c_hbm, s_hbm, row_hbm, col_hbm, out_ref,
    x_ref, c_ref, s_ref, st_ref, row_ref, col_ref, q_vmem, q_smem, index_ref, sign_ref, split_ref, half_ref, table,
    send1, recv1, send2, recv2, send3, recv3,
    sems, send1_sem, recv1_sem, send2_sem, recv2_sem, send3_sem, recv3_sem,
):
    grp = lax.axis_index("grp")
    shard = lax.axis_index("shard")

    def peer1(step):
        group = step >> 2
        depth = jnp.where(group < 4, group, 4 | ((shard & 3) ^ (7 - group)))
        return ((shard + 8 + (step << 3)) & 24) | depth

    copies = [
        pltpu.make_async_copy(row_hbm, row_ref, sems.at[0]),
        pltpu.make_async_copy(col_hbm, col_ref, sems.at[1]),
        pltpu.make_async_copy(s_hbm, s_ref, sems.at[2]),
        pltpu.make_async_copy(x_hbm.at[0], x_ref.at[0], sems.at[3]),
        pltpu.make_async_copy(c_hbm.at[0], c_ref.at[0], sems.at[4]),
        pltpu.make_async_copy(x_hbm.at[1], x_ref.at[1], sems.at[5]),
        pltpu.make_async_copy(c_hbm.at[1], c_ref.at[1], sems.at[6]),
    ]
    for copy in copies:
        copy.start()

    barrier = pltpu.get_barrier_semaphore()

    @pl.when(shard < DIRECT)
    def _():
        for depth in (4, 5, 6, 7, 3, 2, 1, 0):

            def greet_all(n, carry):
                peer = (grp ^ (n >> 2), shard ^ (((n & 3) << 3) | depth))
                pl.semaphore_signal(barrier, inc=1, device_id=peer, device_id_type=MESH)
                return carry

            lax.fori_loop(0 if depth else 1, 4 * SECOND, greet_all, 0, unroll=4 if depth else 1)

    @pl.when(shard >= DIRECT)
    def _():
        def greet(step, carry):
            pl.semaphore_signal(barrier, inc=1, device_id=(grp, shard ^ step), device_id_type=MESH)
            return carry

        def greet_near(step, carry):
            pl.semaphore_signal(barrier, inc=1, device_id=(grp ^ step, shard), device_id_type=MESH)
            return carry

        lax.fori_loop(1, FIRST, greet, 0)
        lax.fori_loop(1, SECOND, greet_near, 0)

    h128 = hadamard((128, 128))
    lanes = lane_transform()

    copies[0].wait()
    copies[1].wait()
    row, col = row_ref[...], col_ref[...]
    device_bits = ((row >> 9) & grp) | (((col >> 9) & shard) << 3)
    entry = ((row & 511) >> 6) * COLS + (col & 511)
    packed = entry | ((row & (NARROW - 1)) << 12) | (parity(device_bits) << 18)
    lane = lax.broadcasted_iota(jnp.int32, (8, 128), 1)
    sublane = lax.broadcasted_iota(jnp.int32, (8, 128), 0)
    ordered = []
    for chunk in range(8):
        at = (chunk % 4) * 2 + chunk // 4
        value = None
        for i in range(SECOND):
            moved = packed[8 * i : 8 * i + 8]
            if i != at:
                moved = pltpu.roll(moved, ((i - at) % 8) * PER_ROW, 1)
            value = moved if value is None else jnp.where(lane // PER_ROW == i, moved, value)
        ordered.append(value)
    packed = jnp.concatenate(ordered, axis=0)
    q_vmem[...] = packed & 4095
    q_copy = pltpu.make_async_copy(q_vmem, q_smem, sems.at[7])
    q_copy.start()
    marks = (((packed >> 12) & (NARROW - 1)) | ((packed >> 18) << 7)).astype(F32)
    mine = (lane // PER_ROW) == sublane

    def diagonal(values):
        blocks = [jnp.where(mine, jnp.broadcast_to(values[r : r + 1], (8, 128)), 0.0) for r in range(64)]
        return jnp.concatenate(blocks, axis=0).astype(BF16)

    found = dot(diagonal(marks), spread_table(128, lambda y: y & (PER_ROW - 1))).astype(jnp.int32)
    for r in range(FIRST):
        second_half = found[8 * (FIRST + r) : 8 * (FIRST + r) + 8]
        mark = jnp.where((lane // PER_ROW) % 2 == 1, second_half, found[8 * r : 8 * r + 8])
        index_ref[r] = (mark & (NARROW - 1)) | (lane & NARROW)
        sign_ref[r] = jnp.where(mark >= 128, -SCALE, SCALE)

    copies[2].wait()
    st_ref[...] = jnp.transpose(s_ref[...].astype(F32))[:UNITS]
    for e in range(EXAMPLES):
        copies[3 + 2 * e].wait()
        copies[4 + 2 * e].wait()
        signed = dot(c_ref[e], x_ref[e]) * st_ref[...]
        t = [signed[:, 128 * j : 128 * j + 128] for j in range(4)]
        a, b, c, d = t[0] + t[1], t[0] - t[1], t[2] + t[3], t[2] - t[3]
        part = slice(128 * e, 128 * e + 128)
        for j, value in enumerate((a + c, b + d, a - c, b - d)):
            for block in range(4):
                rows = slice(128 * block, min(128 * block + 128, UNITS))
                high, low = split(value[rows])
                size = high.shape[0]
                split_ref[j, 256 * block : 256 * block + size, part] = high
                split_ref[j, 256 * block + size : 256 * block + 2 * size, part] = low
    full = jnp.concatenate([h128, h128], axis=1)
    short = jnp.concatenate([h128[:, : UNITS - 384], h128[:, : UNITS - 384]], axis=1)
    for j in range(4):
        t = [dot(full, split_ref[j, 256 * block : 256 * block + 256]) for block in range(3)]
        t.append(dot(short, split_ref[j, 768:]))
        a, b, c, d = t[0] + t[1], t[0] - t[1], t[2] + t[3], t[2] - t[3]
        for block, value in enumerate((a + c, b + d, a - c, b - d)):
            rows = slice(128 * block, 128 * block + 128)
            high, low = split(value)
            half_ref[j, rows, :256] = high
            half_ref[j, rows, 256:] = low
    lanes2 = jnp.concatenate([lanes, lanes], axis=0)
    for j in range(4):
        both = dot(half_ref[j], lanes2)
        table[pl.ds(2 * j * COLS, COLS)] = both[:, :128]
        table[pl.ds((2 * j + 1) * COLS, COLS)] = both[:, 128:]
    q_copy.wait()

    place = lane & (NARROW - 1)

    def pick(target):
        block = ((target & 3) << 3) | (target >> 2)
        index = index_ref[block]
        found = jnp.zeros((8, 128), F32)
        for half in range(2):
            r = block + half * FIRST
            for m in range(PER_ROW):
                rows = None
                for i in range(SECOND):
                    q = q_smem.at[:, pl.ds(i * PER_ROW + m, 1)][r, 0]
                    one = jnp.broadcast_to(table[pl.ds(q, 1), :], (8, 128))
                    rows = one if rows is None else jnp.where(sublane == i, one, rows)
                found = jnp.where(place == half * PER_ROW + m, permute(rows, index), found)
        return found * sign_ref[block]

    def deliver(step, carry):
        target = peer1(step)

        @pl.when((target >= DIRECT) & (target != shard))
        def _():
            pltpu.make_async_remote_copy(
                src_ref=send1.at[step], dst_ref=recv1.at[shard], send_sem=send1_sem, recv_sem=recv1_sem,
                device_id=(grp, target), device_id_type=MESH,
            ).start()

        @pl.when((target >= DIRECT) & (target == shard))
        def _():
            recv1[shard] = send1[step]

        @pl.when(target < DIRECT)
        def _():
            block = send1[step]
            for g in range(SECOND):
                send3[target, g] = block[g : g + 1]

            def row(n, carry):
                g = n ^ 1

                @pl.when((target != shard) | (g != grp))
                def _():
                    pltpu.make_async_remote_copy(
                        src_ref=send3.at[target, g], dst_ref=recv3.at[grp * FIRST + shard], send_sem=send3_sem,
                        recv_sem=recv3_sem, device_id=(g, target), device_id_type=MESH,
                    ).start()

                @pl.when((target == shard) & (g == grp))
                def _():
                    recv3[grp * FIRST + shard] = send3[target, g]

                return carry

            lax.fori_loop(0, SECOND, row, 0)

        return carry

    depth = shard & 7
    meet = jnp.where(depth >= 4, 0, 9 - (5 * depth) // 2)

    def produce(pair, carry):
        first, second = 2 * pair, 2 * pair + 1
        found = pick(peer1(first)), pick(peer1(second))
        send1[first], send1[second] = found

        @pl.when(pair == meet)
        def _():
            pl.semaphore_wait(barrier, FIRST + SECOND - 2 + (SECOND - 1) * jnp.where(shard < DIRECT, DIRECT - 1, DIRECT))

        @pl.when(pair >= meet)
        def _():
            lax.fori_loop(jnp.where(pair == meet, 0, first), second + 1, deliver, 0)

        return carry

    lax.fori_loop(0, FIRST // 2, produce, 0)
    def awaited(buffer, count, semaphore):
        part = buffer.at[pl.ds(0, count)]
        pltpu.make_async_copy(part, part, semaphore).wait()

    def finish(total):
        for e in range(EXAMPLES):
            out_ref[e : e + 1, :] = total[:, NARROW * e : NARROW * e + KEPT // 256]

    @pl.when(shard < DIRECT)
    def _():
        awaited(recv3, FIRST * SECOND - 1, recv3_sem)
        parts = [recv3[n] for n in range(4)]
        for source in range(4, FIRST * SECOND):
            parts[source % 4] = parts[source % 4] + recv3[source]
        finish((parts[0] + parts[1]) + (parts[2] + parts[3]))
        awaited(send1, FIRST - DIRECT, send1_sem)
        awaited(recv3, DIRECT * SECOND - 1, send3_sem)

    @pl.when(shard >= DIRECT)
    def _():
        awaited(recv1, FIRST - 1, recv1_sem)
        total = recv1[0]
        for source in range(1, FIRST):
            total = total + recv1[source]
        for target in range(SECOND):
            send2[target] = total[target : target + 1]
        for target in (1, 0, 2, 3, 6, 7, 4, 5):

            @pl.when(target != grp)
            def _():
                pltpu.make_async_remote_copy(
                    src_ref=send2.at[target], dst_ref=recv2.at[grp], send_sem=send2_sem, recv_sem=recv2_sem,
                    device_id=(target, shard), device_id_type=MESH,
                ).start()

        recv2[grp] = send2[grp]
        awaited(recv2, SECOND - 1, recv2_sem)
        total = recv2[0]
        for source in range(1, SECOND):
            total = total + recv2[source]
        finish(total)
        awaited(send1, FIRST - DIRECT - 1, send1_sem)
        awaited(recv3, DIRECT * SECOND, send3_sem)
        awaited(recv2, SECOND - 1, send2_sem)


def local(inputs, up_cotangent, signs, kept_row, kept_col):
    hbm = pl.BlockSpec(memory_space=pl.ANY)
    return pl.pallas_call(
        kernel,
        out_shape=jax.ShapeDtypeStruct((EXAMPLES, KEPT // 256), F32),
        in_specs=[hbm] * 5,
        out_specs=pl.BlockSpec(memory_space=pltpu.VMEM),
        scratch_shapes=[
            pltpu.VMEM((EXAMPLES, TOKENS, ROWS), BF16),
            pltpu.VMEM((EXAMPLES, UNITS, TOKENS), BF16),
            pltpu.VMEM((ROWS, COLS), jnp.int32),
            pltpu.VMEM((UNITS, ROWS), F32),
            pltpu.VMEM((64, 128), jnp.int32),
            pltpu.VMEM((64, 128), jnp.int32),
            pltpu.VMEM((64, 128), jnp.int32),
            pltpu.SMEM((64, 128), jnp.int32),
            pltpu.VMEM((FIRST, 8, 128), jnp.int32),
            pltpu.VMEM((FIRST, 8, 128), F32),
            pltpu.VMEM((4, 2 * UNITS, 256), BF16),
            pltpu.VMEM((4, COLS, 512), BF16),
            pltpu.VMEM((8 * COLS, 128), F32),
            pltpu.VMEM((FIRST, 8, 128), F32),
            pltpu.VMEM((FIRST, 8, 128), F32),
            pltpu.VMEM((SECOND, 1, 128), F32),
            pltpu.VMEM((SECOND, 1, 128), F32),
            pltpu.VMEM((DIRECT, SECOND, 1, 128), F32),
            pltpu.VMEM((FIRST * SECOND, 1, 128), F32),
            pltpu.SemaphoreType.DMA((8,)),
            pltpu.SemaphoreType.DMA,
            pltpu.SemaphoreType.DMA,
            pltpu.SemaphoreType.DMA,
            pltpu.SemaphoreType.DMA,
            pltpu.SemaphoreType.DMA,
            pltpu.SemaphoreType.DMA,
        ],
        compiler_params=pltpu.CompilerParams(
            vmem_limit_bytes=32 << 20, collective_id=0, has_side_effects=True
        ),
    )(*[
        pltpu.with_memory_space_constraint(array, pltpu.HBM)
        for array in (inputs, jnp.swapaxes(up_cotangent, 1, 2), signs, kept_row.reshape(64, 128), kept_col.reshape(64, 128))
    ])


def solution(mesh):
    placed = (P(None, None, "grp"), P(None, None, "shard"), P("grp", "shard"), P(), P())
    return jax.shard_map(
        local, mesh=mesh, in_specs=placed, out_specs=P(None, ("grp", "shard")), check_vma=False
    )
```

```python
import math

import jax
import jax.numpy as jnp
from jax import lax
from jax.experimental import pallas as pl
from jax.experimental.pallas import tpu as pltpu
from jax.sharding import PartitionSpec as P

F32 = jnp.float32
BF16 = jnp.bfloat16
MESH = pl.DeviceIdType.MESH

EXAMPLES = 2
TOKENS = 1024
ROWS = 512
COLS = 512
UNITS = 448
KEPT = 8192
SCALE = 1.0 / math.sqrt(4096 * 16384)
FIRST = 32
SECOND = 8
DIRECT = 2
NARROW = 64
PER_ROW = 16


def parity(bits):
    for shift in (8, 4, 2, 1):
        bits = bits ^ (bits >> shift)
    return bits & 1


def hadamard(shape):
    row = lax.broadcasted_iota(jnp.int32, shape, 0)
    col = lax.broadcasted_iota(jnp.int32, shape, 1)
    return jnp.where(parity(row & col) == 1, -1.0, 1.0).astype(BF16)


def lane_transform():
    row = lax.broadcasted_iota(jnp.int32, (256, 256), 0)
    col = lax.broadcasted_iota(jnp.int32, (256, 256), 1)
    target = ((col >> 7) << 6) | (col & 63)
    sign = jnp.where(parity((row & 127) & target) == 1, -1.0, 1.0)
    return jnp.where((row >> 7) == ((col >> 6) & 1), sign, 0.0).astype(BF16)


def split(values):
    high = values.astype(BF16)
    return high, (values - high.astype(F32)).astype(BF16)


def permute(values, index):
    numbers = lax.GatherDimensionNumbers(
        offset_dims=(), collapsed_slice_dims=(1,), start_index_map=(1,),
        operand_batching_dims=(0,), start_indices_batching_dims=(0,),
    )
    return lax.gather(values, index[..., None], numbers, (1, 1), mode=lax.GatherScatterMode.PROMISE_IN_BOUNDS)


def spread_table(columns, chosen):
    row = lax.broadcasted_iota(jnp.int32, (128, columns), 0)
    col = lax.broadcasted_iota(jnp.int32, (128, columns), 1)
    return jnp.where((row & (PER_ROW - 1)) == chosen(col), 1.0, 0.0).astype(BF16)


def dot(a, b):
    return jnp.dot(a, b, preferred_element_type=F32)


def kernel(
    x_hbm, c_hbm, s_hbm, row_hbm, col_hbm, out_ref,
    x_ref, c_ref, s_ref, st_ref, row_ref, col_ref, q_vmem, q_smem, index_ref, sign_ref, split_ref, half_ref, table,
    send1, recv1, send2, recv2, send3, recv3,
    sems, send1_sem, recv1_sem, send2_sem, recv2_sem, send3_sem, recv3_sem,
):
    grp = lax.axis_index("grp")
    shard = lax.axis_index("shard")

    def peer1(step):
        group = step >> 2
        depth = jnp.where(group < 4, group, 4 | ((shard & 3) ^ (7 - group)))
        return ((shard + 8 + (step << 3)) & 24) | depth

    copies = [
        pltpu.make_async_copy(row_hbm, row_ref, sems.at[0]),
        pltpu.make_async_copy(col_hbm, col_ref, sems.at[1]),
        pltpu.make_async_copy(s_hbm, s_ref, sems.at[2]),
        pltpu.make_async_copy(x_hbm.at[0], x_ref.at[0], sems.at[3]),
        pltpu.make_async_copy(c_hbm.at[0], c_ref.at[0], sems.at[4]),
        pltpu.make_async_copy(x_hbm.at[1], x_ref.at[1], sems.at[5]),
        pltpu.make_async_copy(c_hbm.at[1], c_ref.at[1], sems.at[6]),
    ]
    for copy in copies:
        copy.start()

    barrier = pltpu.get_barrier_semaphore()

    @pl.when(shard < DIRECT)
    def _():
        for depth in (4, 5, 6, 7, 3, 2, 1, 0):

            def greet_all(n, carry):
                peer = (grp ^ (n >> 2), shard ^ (((n & 3) << 3) | depth))
                pl.semaphore_signal(barrier, inc=1, device_id=peer, device_id_type=MESH)
                return carry

            lax.fori_loop(0 if depth else 1, 4 * SECOND, greet_all, 0, unroll=4 if depth else 1)

    @pl.when(shard >= DIRECT)
    def _():
        def greet(step, carry):
            pl.semaphore_signal(barrier, inc=1, device_id=(grp, shard ^ step), device_id_type=MESH)
            return carry

        def greet_near(step, carry):
            pl.semaphore_signal(barrier, inc=1, device_id=(grp ^ step, shard), device_id_type=MESH)
            return carry

        lax.fori_loop(1, FIRST, greet, 0)
        lax.fori_loop(1, SECOND, greet_near, 0)

    h128 = hadamard((128, 128))
    lanes = lane_transform()

    copies[0].wait()
    copies[1].wait()
    row, col = row_ref[...], col_ref[...]
    device_bits = ((row >> 9) & grp) | (((col >> 9) & shard) << 3)
    entry = ((row & 511) >> 6) * COLS + (col & 511)
    packed = entry | ((row & (NARROW - 1)) << 12) | (parity(device_bits) << 18)
    lane = lax.broadcasted_iota(jnp.int32, (8, 128), 1)
    sublane = lax.broadcasted_iota(jnp.int32, (8, 128), 0)
    ordered = []
    for chunk in range(8):
        at = (chunk % 4) * 2 + chunk // 4
        value = None
        for i in range(SECOND):
            moved = packed[8 * i : 8 * i + 8]
            if i != at:
                moved = pltpu.roll(moved, ((i - at) % 8) * PER_ROW, 1)
            value = moved if value is None else jnp.where(lane // PER_ROW == i, moved, value)
        ordered.append(value)
    packed = jnp.concatenate(ordered, axis=0)
    q_vmem[...] = packed & 4095
    q_copy = pltpu.make_async_copy(q_vmem, q_smem, sems.at[7])
    q_copy.start()
    marks = (((packed >> 12) & (NARROW - 1)) | ((packed >> 18) << 7)).astype(F32)
    mine = (lane // PER_ROW) == sublane

    def diagonal(values):
        blocks = [jnp.where(mine, jnp.broadcast_to(values[r : r + 1], (8, 128)), 0.0) for r in range(64)]
        return jnp.concatenate(blocks, axis=0).astype(BF16)

    found = dot(diagonal(marks), spread_table(128, lambda y: y & (PER_ROW - 1))).astype(jnp.int32)
    for r in range(FIRST):
        second_half = found[8 * (FIRST + r) : 8 * (FIRST + r) + 8]
        mark = jnp.where((lane // PER_ROW) % 2 == 1, second_half, found[8 * r : 8 * r + 8])
        index_ref[r] = (mark & (NARROW - 1)) | (lane & NARROW)
        sign_ref[r] = jnp.where(mark >= 128, -SCALE, SCALE)

    copies[2].wait()
    st_ref[...] = jnp.transpose(s_ref[...].astype(F32))[:UNITS]
    for e in range(EXAMPLES):
        copies[3 + 2 * e].wait()
        copies[4 + 2 * e].wait()
        signed = dot(c_ref[e], x_ref[e]) * st_ref[...]
        t = [signed[:, 128 * j : 128 * j + 128] for j in range(4)]
        a, b, c, d = t[0] + t[1], t[0] - t[1], t[2] + t[3], t[2] - t[3]
        part = slice(128 * e, 128 * e + 128)
        for j, value in enumerate((a + c, b + d, a - c, b - d)):
            for block in range(4):
                rows = slice(128 * block, min(128 * block + 128, UNITS))
                high, low = split(value[rows])
                size = high.shape[0]
                split_ref[j, 256 * block : 256 * block + size, part] = high
                split_ref[j, 256 * block + size : 256 * block + 2 * size, part] = low
    full = jnp.concatenate([h128, h128], axis=1)
    short = jnp.concatenate([h128[:, : UNITS - 384], h128[:, : UNITS - 384]], axis=1)
    for j in range(4):
        t = [dot(full, split_ref[j, 256 * block : 256 * block + 256]) for block in range(3)]
        t.append(dot(short, split_ref[j, 768:]))
        a, b, c, d = t[0] + t[1], t[0] - t[1], t[2] + t[3], t[2] - t[3]
        for block, value in enumerate((a + c, b + d, a - c, b - d)):
            rows = slice(128 * block, 128 * block + 128)
            high, low = split(value)
            half_ref[j, rows, :256] = high
            half_ref[j, rows, 256:] = low
    lanes2 = jnp.concatenate([lanes, lanes], axis=0)
    for j in range(4):
        both = dot(half_ref[j], lanes2)
        table[pl.ds(2 * j * COLS, COLS)] = both[:, :128]
        table[pl.ds((2 * j + 1) * COLS, COLS)] = both[:, 128:]
    q_copy.wait()

    place = lane & (NARROW - 1)

    def pick(target):
        block = ((target & 3) << 3) | (target >> 2)
        index = index_ref[block]
        found = jnp.zeros((8, 128), F32)
        for half in range(2):
            r = block + half * FIRST
            for m in range(PER_ROW):
                rows = None
                for i in range(SECOND):
                    q = q_smem.at[:, pl.ds(i * PER_ROW + m, 1)][r, 0]
                    one = jnp.broadcast_to(table[pl.ds(q, 1), :], (8, 128))
                    rows = one if rows is None else jnp.where(sublane == i, one, rows)
                found = jnp.where(place == half * PER_ROW + m, permute(rows, index), found)
        return found * sign_ref[block]

    def deliver(step, carry):
        target = peer1(step)

        @pl.when((target >= DIRECT) & (target != shard))
        def _():
            pltpu.make_async_remote_copy(
                src_ref=send1.at[step], dst_ref=recv1.at[shard], send_sem=send1_sem, recv_sem=recv1_sem,
                device_id=(grp, target), device_id_type=MESH,
            ).start()

        @pl.when((target >= DIRECT) & (target == shard))
        def _():
            recv1[shard] = send1[step]

        @pl.when(target < DIRECT)
        def _():
            block = send1[step]
            for g in range(SECOND):
                send3[target, g] = block[g : g + 1]

            def row(g):
                return pltpu.make_async_remote_copy(
                    src_ref=send3.at[target, g], dst_ref=recv3.at[grp * FIRST + shard], send_sem=send3_sem,
                    recv_sem=recv3_sem, device_id=(g, target), device_id_type=MESH,
                )

            @pl.when(target != shard)
            def _():
                for g in (1, 0, 3, 2, 5, 4, 7, 6):
                    row(g).start()

            @pl.when(target == shard)
            def _():
                def inner(step, carry):
                    row(grp ^ step).start()
                    return carry

                lax.fori_loop(1, SECOND, inner, 0)
                recv3[grp * FIRST + shard] = send3[target, grp]

        return carry

    depth = shard & 7
    meet = jnp.where(depth >= 4, 0, 12 - 3 * depth)

    def produce(pair, carry):
        first, second = 2 * pair, 2 * pair + 1
        found = pick(peer1(first)), pick(peer1(second))
        send1[first], send1[second] = found

        @pl.when(pair == meet)
        def _():
            pl.semaphore_wait(barrier, FIRST + SECOND - 2 + (SECOND - 1) * jnp.where(shard < DIRECT, DIRECT - 1, DIRECT))

        @pl.when(pair >= meet)
        def _():
            lax.fori_loop(jnp.where(pair == meet, 0, first), second + 1, deliver, 0)

        return carry

    lax.fori_loop(0, FIRST // 2, produce, 0)
    def awaited(buffer, count, semaphore):
        part = buffer.at[pl.ds(0, count)]
        pltpu.make_async_copy(part, part, semaphore).wait()

    def finish(total):
        for e in range(EXAMPLES):
            out_ref[e : e + 1, :] = total[:, NARROW * e : NARROW * e + KEPT // 256]

    @pl.when(shard < DIRECT)
    def _():
        awaited(recv3, FIRST * SECOND - 1, recv3_sem)
        parts = [recv3[n] for n in range(4)]
        for source in range(4, FIRST * SECOND):
            parts[source % 4] = parts[source % 4] + recv3[source]
        finish((parts[0] + parts[1]) + (parts[2] + parts[3]))
        awaited(send1, FIRST - DIRECT, send1_sem)
        awaited(recv3, DIRECT * SECOND - 1, send3_sem)

    @pl.when(shard >= DIRECT)
    def _():
        awaited(recv1, FIRST - 1, recv1_sem)
        total = recv1[0]
        for source in range(1, FIRST):
            total = total + recv1[source]
        for target in range(SECOND):
            send2[target] = total[target : target + 1]
        for target in (1, 0, 2, 3, 6, 7, 4, 5):

            @pl.when(target != grp)
            def _():
                pltpu.make_async_remote_copy(
                    src_ref=send2.at[target], dst_ref=recv2.at[grp], send_sem=send2_sem, recv_sem=recv2_sem,
                    device_id=(target, shard), device_id_type=MESH,
                ).start()

        recv2[grp] = send2[grp]
        awaited(recv2, SECOND - 1, recv2_sem)
        total = recv2[0]
        for source in range(1, SECOND):
            total = total + recv2[source]
        finish(total)
        awaited(send1, FIRST - DIRECT - 1, send1_sem)
        awaited(recv3, DIRECT * SECOND, send3_sem)
        awaited(recv2, SECOND - 1, send2_sem)


def local(inputs, up_cotangent, signs, kept_row, kept_col):
    hbm = pl.BlockSpec(memory_space=pl.ANY)
    return pl.pallas_call(
        kernel,
        out_shape=jax.ShapeDtypeStruct((EXAMPLES, KEPT // 256), F32),
        in_specs=[hbm] * 5,
        out_specs=pl.BlockSpec(memory_space=pltpu.VMEM),
        scratch_shapes=[
            pltpu.VMEM((EXAMPLES, TOKENS, ROWS), BF16),
            pltpu.VMEM((EXAMPLES, UNITS, TOKENS), BF16),
            pltpu.VMEM((ROWS, COLS), jnp.int32),
            pltpu.VMEM((UNITS, ROWS), F32),
            pltpu.VMEM((64, 128), jnp.int32),
            pltpu.VMEM((64, 128), jnp.int32),
            pltpu.VMEM((64, 128), jnp.int32),
            pltpu.SMEM((64, 128), jnp.int32),
            pltpu.VMEM((FIRST, 8, 128), jnp.int32),
            pltpu.VMEM((FIRST, 8, 128), F32),
            pltpu.VMEM((4, 2 * UNITS, 256), BF16),
            pltpu.VMEM((4, COLS, 512), BF16),
            pltpu.VMEM((8 * COLS, 128), F32),
            pltpu.VMEM((FIRST, 8, 128), F32),
            pltpu.VMEM((FIRST, 8, 128), F32),
            pltpu.VMEM((SECOND, 1, 128), F32),
            pltpu.VMEM((SECOND, 1, 128), F32),
            pltpu.VMEM((DIRECT, SECOND, 1, 128), F32),
            pltpu.VMEM((FIRST * SECOND, 1, 128), F32),
            pltpu.SemaphoreType.DMA((8,)),
            pltpu.SemaphoreType.DMA,
            pltpu.SemaphoreType.DMA,
            pltpu.SemaphoreType.DMA,
            pltpu.SemaphoreType.DMA,
            pltpu.SemaphoreType.DMA,
            pltpu.SemaphoreType.DMA,
        ],
        compiler_params=pltpu.CompilerParams(
            vmem_limit_bytes=32 << 20, collective_id=0, has_side_effects=True
        ),
    )(*[
        pltpu.with_memory_space_constraint(array, pltpu.HBM)
        for array in (inputs, jnp.swapaxes(up_cotangent, 1, 2), signs, kept_row.reshape(64, 128), kept_col.reshape(64, 128))
    ])


def solution(mesh):
    placed = (P(None, None, "grp"), P(None, None, "shard"), P("grp", "shard"), P(), P())
    return jax.shard_map(
        local, mesh=mesh, in_specs=placed, out_specs=P(None, ("grp", "shard")), check_vma=False
    )
```
